256 devices in a mesh: gx: 32 (over z, y_hi, core), gy: 8 (over y_lo, x).
Axes of the slice: x: 4, y: 4 (y_hi: 2, y_lo: 2; y = y_hi * 2 + y_lo), z: 8, core: 2. Of those that a mesh axis runs over, the one named last changes fastest.
Arguments:
- features: float32 [32, 8, 24, 64, 128], P('gx', 'gy'), may hold values from -6 to 6
- weights: float32 [27, 64, 64], replicated, may hold values from -0.15625 to 0.15625
- kernel_map: int32 [32, 8, 24, 27], P('gx', 'gy'), may hold values from 0 to 56, as said below
- send_lists: int32 [32, 8, 8, 4], P('gx', 'gy'), may hold values from 0 to 23, as said below
- counts: int32 [32, 8], P('gx', 'gy'), may hold values from 6 to 24, as said below
- cotangent: float32 [32, 8, 24, 64, 128], P('gx', 'gy'), may hold values from -6 to 6
Outputs:
- activations: float32 [32, 8, 24, 64, 128], P('gx', 'gy')
- grad_features: float32 [32, 8, 24, 64, 128], P('gx', 'gy')
- grad_weights: float32 [27, 64, 64], replicated
The draws below stay inside these ranges and needn't reach their ends.
Inputs may be any that keep to these rules, and one draw needn't show every extreme that they name: `counts`: some device has exactly 24 occupied slots. `send_lists`: every entry names an occupied tile slot of the sending device, below its count. `kernel_map`: entries below 24 name slots of the device itself; offset 13 of slot t is t; entry 24 + r * 4 + h is entry h of halo block r; entry 24 + 32 is the empty tile.
All inputs are finite; a program needn't handle non-finite values.
Results may differ from the reference program's by a relative error of at most 0.0003.
Values sent between devices are 32-bit elements; how exact they have to be, the bound alone decides.
A program may use at most 64 MiB of HBM per device.

```python
import jax
import jax.numpy as jnp
from jax import lax

C = 64
V = 128
TILES = 24
HALO = 4
OFFS = 27
N_GX = 32
N_GY = 8


def tile_counts(key):
    inner = jax.random.fold_in(key, 101)
    flat = jax.random.randint(inner, (N_GX * N_GY,), TILES // 4, TILES + 1)
    place = jax.random.randint(jax.random.fold_in(inner, 1), (), 0, N_GX * N_GY)
    flat = flat.at[place].set(TILES)
    return flat.reshape(N_GX, N_GY).astype(jnp.int32)


def draw_counts(key, part):
    return tile_counts(key)


def draw_send_lists(key, part):
    occupied = tile_counts(key)
    key = jax.random.fold_in(key, 3)
    raw = jax.random.randint(key, (N_GX, N_GY, 8, HALO), 0, 1 << 20)
    result = (raw % occupied[:, :, None, None]).astype(jnp.int32)
    result = result.at[:, :, 0, 0].set(occupied - 1)
    result = result.at[:, :, 7, 0].set(0)
    return result.astype(jnp.int32)


def draw_kernel_map(key, part):
    occupied = tile_counts(key)
    key = jax.random.fold_in(key, 5)
    first, second, third = jax.random.split(key, 3)
    shape = (N_GX, N_GY, TILES, OFFS)
    kind = jax.random.randint(first, shape, 0, 10)
    local = jax.random.randint(second, shape, 0, 1 << 20) % occupied[:, :, None, None]
    remote = TILES + jax.random.randint(third, shape, 0, 8 * HALO)
    empty = jnp.full(shape, TILES + 8 * HALO, jnp.int32)
    result = jnp.where(kind < 3, empty, jnp.where(kind < 7, local, remote))
    centre = jnp.broadcast_to(jnp.arange(TILES, dtype=jnp.int32)[None, None, :], (N_GX, N_GY, TILES))
    result = result.at[:, :, :, 13].set(centre)
    return result.astype(jnp.int32)


def block_levels(rng, extent, cuts, smallest, top_value):
    level, own = 1.0, jax.random.fold_in(rng, 6)
    for axis_at, parts in cuts:
        heights = jnp.exp(jax.random.uniform(jax.random.fold_in(own, axis_at), (parts,), jnp.float32, smallest / len(cuts), top_value / len(cuts)))
        level = level * jnp.repeat(heights, extent[axis_at] // parts).reshape([-1 if axis == axis_at else 1 for axis in range(len(extent))])
    return level


def normal_values(stream_key, extent, spread, reach, shards=(), kind=jnp.bfloat16):
    values = jax.random.normal(stream_key, extent, jnp.float32) * spread
    if len(shards) > 0:
        values = block_levels(stream_key, extent, shards, -0.22, 0.18) * values
    return jnp.clip(values, min=-reach, max=reach).astype(kind)


def setup_inputs(seed: int = 0) -> dict:
    splits = jax.random.split(jax.random.key(seed), 7)
    features = normal_values(splits[0], (N_GX, N_GY, TILES, C, V), 1.0, 6.0, ((0, 32), (1, 8)), jnp.float32)
    weights = normal_values(splits[1], (OFFS, C, C), (OFFS * C) ** -0.5, 0.15625, (), jnp.float32)
    kernel_map = draw_kernel_map(jax.random.fold_in(splits[6], 71), 0)
    send_lists = draw_send_lists(jax.random.fold_in(splits[6], 71), 0)
    counts = draw_counts(jax.random.fold_in(splits[6], 71), 0)
    cotangent = normal_values(splits[5], (N_GX, N_GY, TILES, C, V), 1.0, 6.0, ((0, 32), (1, 8)), jnp.float32)
    return dict(features=features, weights=weights, kernel_map=kernel_map, send_lists=send_lists, counts=counts, cotangent=cotangent)


OFFSETS = ((-1, -1), (-1, 0), (-1, 1), (0, -1), (0, 1), (1, -1), (1, 0), (1, 1))


def device_pass(extended, kmap, grad_out, count, weights):
    tiles = kmap.shape[0]
    live = (lax.iota(jnp.int32, tiles) < count).astype(jnp.float32)[:, None, None]

    def forward(total, item):
        w_k, column = item
        picked = extended[column]
        return total + jnp.einsum("oc,tcv->tov", w_k, picked, precision=lax.Precision.HIGHEST), None

    start = jnp.zeros((tiles, extended.shape[1], extended.shape[2]), jnp.float32)
    pre, _ = lax.scan(forward, start, (weights, kmap.T))
    sig = jax.nn.sigmoid(pre)
    act = pre * sig * live
    grad_pre = grad_out * live * sig * (1.0 + pre * (1.0 - sig))

    def backward(acc, item):
        w_k, column = item
        picked = extended[column]
        g_w = jnp.einsum("tov,tcv->oc", grad_pre, picked, precision=lax.Precision.HIGHEST)
        contrib = jnp.einsum("oc,tov->tcv", w_k, grad_pre, precision=lax.Precision.HIGHEST)
        return acc.at[column].add(contrib), g_w

    grad_ext, grad_w = lax.scan(backward, jnp.zeros_like(extended), (weights, kmap.T))
    return act, grad_w, grad_ext


def pick_rows(source, index):
    return source[index]


def add_rows(target, index, values):
    return target.at[index].add(values)


def reference(features, weights, kernel_map, send_lists, counts, cotangent):
    grid_x, grid_y = N_GX, N_GY
    devices = grid_x * grid_y
    tiles = features.shape[2]
    halo = send_lists.shape[3]
    chan = features.shape[3]
    vox = features.shape[4]
    padded = jnp.pad(features, ((1, 1), (1, 1), (0, 0), (0, 0), (0, 0)))
    sends_pad = jnp.pad(send_lists, ((1, 1), (1, 1), (0, 0), (0, 0)))
    pieces = [features]
    for slot, (step_x, step_y) in enumerate(OFFSETS):
        source = padded[1 + step_x:1 + step_x + grid_x, 1 + step_y:1 + step_y + grid_y]
        chosen = sends_pad[1 + step_x:1 + step_x + grid_x, 1 + step_y:1 + step_y + grid_y, slot]
        block = jax.vmap(pick_rows)(source.reshape(devices, tiles, chan, vox), chosen.reshape(devices, halo))
        pieces.append(block.reshape(grid_x, grid_y, halo, chan, vox))
    pieces.append(jnp.zeros((grid_x, grid_y, 1, chan, vox), jnp.float32))
    extended = jnp.concatenate(pieces, axis=2)
    width = extended.shape[2]
    act, grad_w, grad_ext = lax.map(
        lambda item: device_pass(item[0], item[1], item[2], item[3], weights),
        (extended.reshape(devices, width, chan, vox), kernel_map.reshape(devices, tiles, -1),
         cotangent.reshape(devices, tiles, chan, vox), counts.reshape(devices)))
    grad_weights = jnp.sum(grad_w, axis=0)
    grad_ext = grad_ext.reshape(grid_x, grid_y, width, chan, vox)
    grad_x = grad_ext[:, :, :tiles].reshape(devices, tiles, chan, vox)
    for slot, (step_x, step_y) in enumerate(OFFSETS):
        block = grad_ext[:, :, tiles + slot * halo:tiles + (slot + 1) * halo]
        block_pad = jnp.pad(block, ((1, 1), (1, 1), (0, 0), (0, 0), (0, 0)))
        incoming = block_pad[1 - step_x:1 - step_x + grid_x, 1 - step_y:1 - step_y + grid_y]
        grad_x = jax.vmap(add_rows)(grad_x, send_lists[:, :, slot].reshape(devices, halo),
                                    incoming.reshape(devices, halo, chan, vox))
    activations = act.reshape(grid_x, grid_y, tiles, chan, vox)
    return activations, grad_x.reshape(grid_x, grid_y, tiles, chan, vox), grad_weights
```

```python
import jax
import jax.numpy as jnp
from jax import lax
from jax.experimental import pallas as pl
from jax.experimental.pallas import tpu as pltpu
from jax.sharding import PartitionSpec as P

OFFSETS = ((-1, -1), (-1, 0), (-1, 1), (0, -1), (0, 1), (1, -1), (1, 0), (1, 1))
NX, NY = 32, 8
TILES, HALO, OFFS, C, V = 24, 4, 27, 64, 128
WIDE = TILES + 8 * HALO + 1
KC = 28 * C
NB = KC // 128
GROUP, FAR = 8, 32
MESH = pl.DeviceIdType.MESH
F32, BF16 = jnp.float32, jnp.bfloat16
VMEM = pl.BlockSpec(memory_space=pltpu.VMEM)
SMEM = pl.BlockSpec(memory_space=pltpu.SMEM)


def position():
    return lax.axis_index("gx"), lax.axis_index("gy")


def beside(gx, gy, dx, dy):
    return lax.rem(gx + (dx + NX), NX), lax.rem(gy + (dy + NY), NY)


def inside(gx, gy, dx, dy):
    ok = (gx + dx >= 0) & (gx + dx < NX) & (gy + dy >= 0) & (gy + dy < NY)
    return jnp.where(ok, 1.0, 0.0).astype(F32)


def halves(value):
    high = value.astype(BF16)
    return high, (value - high.astype(F32)).astype(BF16)


def near_rank(gx, gy):
    return lax.rem(gy, 4) * 2 + lax.rem(gx, 2)


def far_rank(gx, gy):
    return (gx // 4) * 4 + lax.rem(gx // 2, 2) * 2 + gy // 4


def device_at(near, far):
    gx = (far // 4) * 4 + lax.rem(far // 2, 2) * 2 + lax.rem(near, 2)
    return gx, lax.rem(far, 2) * 4 + near // 2


def fetch_kernel(sends, feat, weights, xh, xl, wcat, wback, outbox, inbox, send_sem, recv_sem):
    gx, gy = position()
    barrier = pltpu.get_barrier_semaphore()
    for dx, dy in OFFSETS:
        pl.semaphore_signal(barrier, inc=1, device_id=beside(gx, gy, dx, dy), device_id_type=MESH)
    pl.semaphore_wait(barrier, 8)
    copies = []
    for r, (dx, dy) in enumerate(OFFSETS):
        for h in range(HALO):
            outbox[r * HALO + h] = feat[0, 0, sends[0, 0, r, h]]
        copy = pltpu.make_async_remote_copy(
            src_ref=outbox.at[pl.ds(r * HALO, HALO)],
            dst_ref=inbox.at[pl.ds(r * HALO, HALO)],
            send_sem=send_sem.at[r],
            recv_sem=recv_sem.at[r],
            device_id=beside(gx, gy, -dx, -dy),
            device_id_type=MESH,
        )
        copy.start()
        copies.append(copy)

    def split_tile(t, carry):
        xh[t], xl[t] = halves(feat[0, 0, t])
        return carry

    lax.fori_loop(0, TILES, split_tile, 0)
    xh[WIDE - 1] = jnp.zeros((C, V), BF16)
    xl[WIDE - 1] = jnp.zeros((C, V), BF16)
    for m in range(NB):
        left = weights[2 * m]
        right = weights[2 * m + 1] if 2 * m + 1 < OFFS else jnp.zeros((C, C), F32)
        pair = jnp.concatenate([left, right], axis=1)
        high, low = halves(pair)
        wcat[0:C, m * 128 : m * 128 + 128] = high
        wcat[C : 2 * C, m * 128 : m * 128 + 128] = low
        turned = pair.T
        high = turned.astype(BF16).astype(F32)
        both = jnp.concatenate([high, turned - high], axis=1).astype(BF16)
        wback[m * 128 : m * 128 + 128, 0:128] = both
        wback[m * 128 : m * 128 + 128, 128:256] = both
    for r, (dx, dy) in enumerate(OFFSETS):
        copies[r].wait_recv()
        there = inside(gx, gy, dx, dy)
        for h in range(HALO):
            slot = r * HALO + h
            xh[TILES + slot], xl[TILES + slot] = halves(inbox[slot] * there)
    for copy in copies:
        copy.wait_send()


def tile_kernel(kmap, counts, xh, xl, wcat, wback, cot, act, ge, gw, catch, catl, total):
    ge[...] = jnp.zeros_like(ge)
    total[...] = jnp.zeros_like(total)
    catch[OFFS * C : KC, :] = jnp.zeros((C, 2 * V), BF16)
    catl[OFFS * C : KC, :] = jnp.zeros((C, 2 * V), BF16)
    contract_last = (((1,), (1,)), ((), ()))

    def pair(p, carry):
        slots = [[kmap[0, 0, 2 * p + h, k] for h in range(2)] for k in range(OFFS)]
        for k in range(OFFS):
            for h in range(2):
                catch[k * C : k * C + C, h * V : h * V + V] = xh[slots[k][h]]
                catl[k * C : k * C + C, h * V : h * V + V] = xl[slots[k][h]]
        first = jnp.dot(wcat[...], catch[...], preferred_element_type=F32)
        second = jnp.dot(wcat[0:C, :], catl[...], preferred_element_type=F32)
        pre = first[0:C] + first[C:] + second
        sig = jax.nn.sigmoid(pre)
        slope = sig * (1.0 + pre * (1.0 - sig))
        value = pre * sig
        grads = []
        for h in range(2):
            live = jnp.where(2 * p + h < counts[0, 0], 1.0, 0.0).astype(F32)
            act[2 * p + h] = value[:, h * V : h * V + V] * live
            grads.append(cot[0, 0, 2 * p + h] * live * slope[:, h * V : h * V + V])
        gh, gl = halves(jnp.concatenate(grads, axis=1))
        two = lax.dot_general(
            jnp.concatenate([gh, gl], axis=0), catch[...], contract_last, preferred_element_type=F32
        )
        one = lax.dot_general(gh, catl[...], contract_last, preferred_element_type=F32)
        total[...] += two[0:C] + two[C:] + one
        four = jnp.concatenate([gh, gh, gl, gl], axis=0)
        for k in range(OFFS):
            part = jnp.dot(wback[k * C : k * C + C, :], four, preferred_element_type=F32)
            for h in range(2):
                ge[slots[k][h]] += part[:, h * V : h * V + V]
        return carry

    lax.fori_loop(0, TILES // 2, pair, 0)
    for j in range(GROUP):
        gw[j] = total[j * 8 : j * 8 + 8, :]


def return_kernel(ge, gw, back, out, near_in, part, far_in, full, halo_s, halo_r, near_s, near_r, far_s, far_r, spread_s, spread_r, end_s, end_r):
    gx, gy = position()
    near, far = near_rank(gx, gy), far_rank(gx, gy)

    def near_device(d):
        return device_at(lax.rem(near + d, GROUP), far)

    def far_device(d):
        return device_at(near, lax.rem(far + d, FAR))

    barrier = pltpu.get_barrier_semaphore()

    def greet_near(d, carry):
        pl.semaphore_signal(barrier, inc=1, device_id=near_device(d), device_id_type=MESH)
        return carry

    def greet_far(d, carry):
        pl.semaphore_signal(barrier, inc=1, device_id=far_device(d), device_id_type=MESH)
        return carry

    for dx, dy in OFFSETS:
        pl.semaphore_signal(barrier, inc=1, device_id=beside(gx, gy, dx, dy), device_id_type=MESH)
    lax.fori_loop(1, GROUP, greet_near, 0)
    lax.fori_loop(1, FAR, greet_far, 0)
    pl.semaphore_wait(barrier, 8 + GROUP - 1 + FAR - 1)

    def near_copy(d):
        return pltpu.make_async_remote_copy(
            src_ref=gw.at[lax.rem(near + d, GROUP)],
            dst_ref=near_in.at[d],
            send_sem=near_s.at[d],
            recv_sem=near_r.at[d],
            device_id=near_device(d),
            device_id_type=MESH,
        )

    def far_copy(d):
        return pltpu.make_async_remote_copy(
            src_ref=part.at[lax.rem(far + d, FAR) // 2],
            dst_ref=far_in.at[d],
            send_sem=far_s.at[d],
            recv_sem=far_r.at[d],
            device_id=far_device(d),
            device_id_type=MESH,
        )

    def spread_copy(d, i):
        return pltpu.make_async_remote_copy(
            src_ref=full.at[i],
            dst_ref=full.at[i],
            send_sem=spread_s.at[d],
            recv_sem=spread_r.at[i],
            device_id=far_device(d),
            device_id_type=MESH,
        )

    def end_copy(d):
        return pltpu.make_async_remote_copy(
            src_ref=full,
            dst_ref=out.at[near],
            send_sem=end_s.at[d],
            recv_sem=end_r.at[d],
            device_id=near_device(d),
            device_id_type=MESH,
        )

    def reduces(rank):
        return (lax.rem(rank, 2) == 0) & (rank < 2 * NB)

    def each(low, high, act):
        def step(d, carry):
            act(d)
            return carry

        lax.fori_loop(low, high, step, 0)

    each(1, GROUP, lambda d: near_copy(d).start())
    halo = []
    for r, (dx, dy) in enumerate(OFFSETS):
        copy = pltpu.make_async_remote_copy(
            src_ref=ge.at[pl.ds(TILES + r * HALO, HALO)],
            dst_ref=back.at[pl.ds(r * HALO, HALO)],
            send_sem=halo_s.at[r],
            recv_sem=halo_r.at[r],
            device_id=beside(gx, gy, dx, dy),
            device_id_type=MESH,
        )
        copy.start()
        halo.append(copy)

    each(1, GROUP, lambda d: near_copy(d).wait_recv())
    mine = gw[near]
    for d in range(1, GROUP):
        mine = mine + near_in[d]
    for i in range(NB):
        part[i] = mine[:, i * 128 : i * 128 + 128]

    def if_other_reduces(d, act):
        pl.when(reduces(lax.rem(far + d, FAR)))(act)

    each(1, FAR, lambda d: if_other_reduces(d, lambda: far_copy(d).start()))

    own = lax.rem(far // 2, NB)

    @pl.when(reduces(far))
    def _():
        each(1, FAR, lambda d: far_copy(d).wait_recv())

        def add(d, acc):
            return acc + far_in[d]

        full[own] = lax.fori_loop(1, FAR, add, part[own])
        each(1, FAR, lambda d: spread_copy(d, own).start())

    def arrived(i):
        pl.when(2 * i != far)(lambda: spread_copy(1, i).wait_recv())

    each(0, NB, arrived)
    each(1, GROUP, lambda d: end_copy(d).start())
    out[near] = full[...]
    each(1, GROUP, lambda d: near_copy(d).wait_send())
    each(1, FAR, lambda d: if_other_reduces(d, lambda: far_copy(d).wait_send()))
    pl.when(reduces(far))(lambda: each(1, FAR, lambda d: spread_copy(d, own).wait_send()))
    for copy in halo:
        copy.wait()
    each(1, GROUP, lambda d: end_copy(d).wait())


def finish_kernel(sends, ge, back, summed, gf, gwo):
    gx, gy = position()
    gf[...] = ge[0:TILES]
    for r, (dx, dy) in enumerate(OFFSETS):
        there = inside(gx, gy, -dx, -dy)
        for h in range(HALO):
            gf[sends[0, 0, r, h]] += back[r * HALO + h] * there
    for j in range(GROUP):
        for i in range(NB):
            block = summed[j, i]
            gwo[2 * i, j * 8 : j * 8 + 8, :] = block[:, 0:C]
            if 2 * i + 1 < OFFS:
                gwo[2 * i + 1, j * 8 : j * 8 + 8, :] = block[:, C : 2 * C]


def shaped(shape, dtype=F32):
    return jax.ShapeDtypeStruct(shape, dtype)


def run_tiles(kernel_map, counts, xh, xl, wcat, wback, cotangent):
    return pl.pallas_call(
        tile_kernel,
        out_shape=(shaped((TILES, C, V)), shaped((WIDE, C, V)), shaped((GROUP, 8, KC))),
        in_specs=[SMEM, SMEM] + [VMEM] * 5,
        out_specs=(VMEM,) * 3,
        scratch_shapes=[
            pltpu.VMEM((KC, 2 * V), BF16),
            pltpu.VMEM((KC, 2 * V), BF16),
            pltpu.VMEM((C, KC), F32),
        ],
        compiler_params=pltpu.CompilerParams(vmem_limit_bytes=32 << 20),
    )(kernel_map, counts, xh, xl, wcat, wback, cotangent)


def per_device(features, weights, kernel_map, send_lists, counts, cotangent):
    dma = pltpu.SemaphoreType.DMA
    xh, xl, wcat, wback = pl.pallas_call(
        fetch_kernel,
        out_shape=(
            shaped((WIDE, C, V), BF16),
            shaped((WIDE, C, V), BF16),
            shaped((2 * C, KC), BF16),
            shaped((KC, 4 * C), BF16),
        ),
        in_specs=[SMEM, VMEM, VMEM],
        out_specs=(VMEM,) * 4,
        scratch_shapes=[
            pltpu.VMEM((8 * HALO, C, V), F32),
            pltpu.VMEM((8 * HALO, C, V), F32),
            dma((8,)),
            dma((8,)),
        ],
        compiler_params=pltpu.CompilerParams(collective_id=0, has_side_effects=True, vmem_limit_bytes=24 << 20),
    )(send_lists, features, weights)
    act, ge, gw = run_tiles(kernel_map, counts, xh, xl, wcat, wback, cotangent)
    back, summed = pl.pallas_call(
        return_kernel,
        out_shape=(shaped((8 * HALO, C, V)), shaped((GROUP, NB, 8, 128))),
        in_specs=[VMEM, VMEM],
        out_specs=(VMEM, VMEM),
        scratch_shapes=[
            pltpu.VMEM((GROUP, 8, KC), F32),
            pltpu.VMEM((16, 8, 128), F32),
            pltpu.VMEM((FAR, 8, 128), F32),
            pltpu.VMEM((NB, 8, 128), F32),
            dma((8,)),
            dma((8,)),
            dma((GROUP,)),
            dma((GROUP,)),
            dma((FAR,)),
            dma((FAR,)),
            dma((FAR,)),
            dma((NB,)),
            dma((GROUP,)),
            dma((GROUP,)),
        ],
        compiler_params=pltpu.CompilerParams(collective_id=1, has_side_effects=True, vmem_limit_bytes=24 << 20),
    )(ge, gw)
    gf, gwo = pl.pallas_call(
        finish_kernel,
        out_shape=(shaped((TILES, C, V)), shaped((OFFS, C, C))),
        in_specs=[SMEM, VMEM, VMEM, VMEM],
        out_specs=(VMEM, VMEM),
        compiler_params=pltpu.CompilerParams(vmem_limit_bytes=24 << 20),
    )(send_lists, ge, back, summed)
    return act[None, None], gf[None, None], gwo


def solution(mesh):
    placed = (
        P("gx", "gy", None, None, None),
        P(),
        P("gx", "gy", None, None),
        P("gx", "gy", None, None),
        P("gx", "gy"),
        P("gx", "gy", None, None, None),
    )
    return jax.shard_map(
        per_device,
        mesh=mesh,
        in_specs=placed,
        out_specs=(P("gx", "gy", None, None, None), P("gx", "gy", None, None, None), P()),
        check_vma=False,
    )
```

```python
import jax
import jax.numpy as jnp
from jax import lax
from jax.experimental import pallas as pl
from jax.experimental.pallas import tpu as pltpu
from jax.sharding import PartitionSpec as P

OFFSETS = ((-1, -1), (-1, 0), (-1, 1), (0, -1), (0, 1), (1, -1), (1, 0), (1, 1))
NX, NY = 32, 8
TILES, HALO, OFFS, C, V = 24, 4, 27, 64, 128
WIDE = TILES + 8 * HALO + 1
KC = 28 * C
NB = KC // 128
PLANE, DEEP, PAIRS = 16, 8, 2
MESH = pl.DeviceIdType.MESH
F32, BF16 = jnp.float32, jnp.bfloat16
VMEM = pl.BlockSpec(memory_space=pltpu.VMEM)
ANY = pl.BlockSpec(memory_space=pl.ANY)
SMEM = pl.BlockSpec(memory_space=pltpu.SMEM)


def position():
    return lax.axis_index("gx"), lax.axis_index("gy")


def beside(gx, gy, dx, dy):
    return lax.rem(gx + (dx + NX), NX), lax.rem(gy + (dy + NY), NY)


def inside(gx, gy, dx, dy):
    ok = (gx + dx >= 0) & (gx + dx < NX) & (gy + dy >= 0) & (gy + dy < NY)
    return jnp.where(ok, 1.0, 0.0).astype(F32)


def halves(value):
    high = value.astype(BF16)
    return high, (value - high.astype(F32)).astype(BF16)


def fetch_kernel(sends, feat_hbm, weights_hbm, xh, xl, wcat, wback, feat, weights, outbox, inbox, load_sem, send_sem, recv_sem):
    gx, gy = position()
    load_feat = pltpu.make_async_copy(feat_hbm.at[0, 0], feat, load_sem.at[0])
    load_weights = pltpu.make_async_copy(weights_hbm, weights, load_sem.at[1])
    load_feat.start()
    load_weights.start()
    barrier = pltpu.get_barrier_semaphore()
    for dx, dy in OFFSETS:
        pl.semaphore_signal(barrier, inc=1, device_id=beside(gx, gy, dx, dy), device_id_type=MESH)
    load_feat.wait()
    for r in range(8):
        for h in range(HALO):
            outbox[r * HALO + h] = feat[sends[0, 0, r, h]]
    pl.semaphore_wait(barrier, 8)
    copies = []
    for r, (dx, dy) in enumerate(OFFSETS):
        copy = pltpu.make_async_remote_copy(
            src_ref=outbox.at[pl.ds(r * HALO, HALO)],
            dst_ref=inbox.at[pl.ds(r * HALO, HALO)],
            send_sem=send_sem.at[r],
            recv_sem=recv_sem.at[r],
            device_id=beside(gx, gy, -dx, -dy),
            device_id_type=MESH,
        )
        copy.start()
        copies.append(copy)
    load_weights.wait()

    def split_tile(t, carry):
        xh[t], xl[t] = halves(feat[t])
        return carry

    lax.fori_loop(0, TILES, split_tile, 0)
    xh[WIDE - 1] = jnp.zeros((C, V), BF16)
    xl[WIDE - 1] = jnp.zeros((C, V), BF16)
    for m in range(NB):
        left = weights[2 * m]
        right = weights[2 * m + 1] if 2 * m + 1 < OFFS else jnp.zeros((C, C), F32)
        pair = jnp.concatenate([left, right], axis=1)
        high, low = halves(pair)
        wcat[0:C, m * 128 : m * 128 + 128] = high
        wcat[C : 2 * C, m * 128 : m * 128 + 128] = low
        turned = pair.T
        high = turned.astype(BF16).astype(F32)
        both = jnp.concatenate([high, turned - high], axis=1).astype(BF16)
        wback[m * 128 : m * 128 + 128, 0:128] = both
        wback[m * 128 : m * 128 + 128, 128:256] = both
    for r, (dx, dy) in enumerate(OFFSETS):
        copies[r].wait_recv()
        there = inside(gx, gy, dx, dy)
        for h in range(HALO):
            slot = r * HALO + h
            xh[TILES + slot], xl[TILES + slot] = halves(inbox[slot] * there)
    for copy in copies:
        copy.wait_send()


def tile_kernel(kmap, counts, xh, xl, wcat, wback, cot, act, ge, g2, catch, catl):
    ge[...] = jnp.zeros_like(ge)
    for q in range(PAIRS):
        catch[q, OFFS * C : KC, :] = jnp.zeros((C, 2 * V), BF16)
        catl[q, OFFS * C : KC, :] = jnp.zeros((C, 2 * V), BF16)

    def step(p, carry):
        def tile(q, h):
            return (p * PAIRS + q) * 2 + h

        slots = [[[kmap[0, 0, tile(q, h), k] for h in range(2)] for k in range(OFFS)] for q in range(PAIRS)]
        for q in range(PAIRS):
            for k in range(OFFS):
                for h in range(2):
                    catch[q, k * C : k * C + C, h * V : h * V + V] = xh[slots[q][k][h]]
                    catl[q, k * C : k * C + C, h * V : h * V + V] = xl[slots[q][k][h]]
        sums = []
        for q in range(PAIRS):
            first = jnp.dot(wcat[...], catch[q], preferred_element_type=F32)
            second = jnp.dot(wcat[0:C, :], catl[q], preferred_element_type=F32)
            sums.append(first[0:C] + first[C:] + second)
        fours = []
        for q in range(PAIRS):
            pre = sums[q]
            sig = jax.nn.sigmoid(pre)
            slope = sig * (1.0 + pre * (1.0 - sig))
            value = pre * sig
            grads = []
            for h in range(2):
                live = jnp.where(tile(q, h) < counts[0, 0], 1.0, 0.0).astype(F32)
                act[tile(q, h)] = value[:, h * V : h * V + V] * live
                grads.append(cot[0, 0, tile(q, h)] * live * slope[:, h * V : h * V + V])
            gh, gl = halves(jnp.concatenate(grads, axis=1))
            lanes = pl.ds(pl.multiple_of((p * PAIRS + q) * 2 * V, 2 * V), 2 * V)
            g2[0:C, lanes] = gh
            g2[C : 2 * C, lanes] = gl
            fours.append(jnp.concatenate([gh, gh, gl, gl], axis=0))
        for q in range(PAIRS):
            for k in range(OFFS):
                part = jnp.dot(wback[k * C : k * C + C, :], fours[q], preferred_element_type=F32)
                for h in range(2):
                    ge[slots[q][k][h]] += part[:, h * V : h * V + V]
        return carry

    lax.fori_loop(0, TILES // (2 * PAIRS), step, 0)


def return_kernel(kmap, xh, xl, g2, ge, back, out, cath, catl, mine, theirs, given, summed, xy_in, z_in, half, halo_s, halo_r, core_s, core_r, xy_s, xy_r, z_s, z_r, spread_s, spread_r, end_s, end_r):
    gx, gy = position()
    core, z = lax.rem(gx, 2), gx // 4
    xy = (lax.rem(gx // 2, 2) * 2 + gy // 4) * 4 + lax.rem(gy, 4)

    def xy_device(u):
        return (z * 4 + (u // 8) * 2 + core, lax.rem(u // 4, 2) * 4 + lax.rem(u, 4))

    def z_device(d):
        return (lax.rem(z + d, DEEP) * 4 + lax.rem(gx, 4), gy)

    other = (gx + 1 - 2 * core, gy)
    barrier = pltpu.get_barrier_semaphore()

    def greet(device):
        pl.semaphore_signal(barrier, inc=1, device_id=device, device_id_type=MESH)

    for dx, dy in OFFSETS:
        greet(beside(gx, gy, dx, dy))
    greet(other)
    for u in range(PLANE):
        pl.when(xy != u)(lambda u=u: greet(xy_device(u)))
    for d in range(1, DEEP):
        greet(z_device(d))

    def send(src, dst, send_sem, recv_sem, device):
        return pltpu.make_async_remote_copy(
            src_ref=src, dst_ref=dst, send_sem=send_sem, recv_sem=recv_sem, device_id=device, device_id_type=MESH
        )

    def core_copy(n):
        return send(theirs.at[n], given.at[n], core_s.at[n], core_r.at[n], other)

    def xy_copy(m, source, target):
        return send(summed.at[m], xy_in.at[source], xy_s.at[m], xy_r.at[source], xy_device(target))

    def z_copy(d, slot):
        return send(z_in.at[slot], z_in.at[slot], z_s.at[d], z_r.at[slot], z_device(d))

    def spread_copy(m, target):
        return send(half.at[m], half.at[m], spread_s.at[target], spread_r.at[m], xy_device(target))

    def compute(n):
        for kk in range(4):
            k = jnp.minimum(4 * n + kk, OFFS - 1)
            for t in range(TILES):
                slot = kmap[0, 0, t, k]
                cath[kk * C : kk * C + C, t * V : t * V + V] = xh[slot]
                catl[kk * C : kk * C + C, t * V : t * V + V] = xl[slot]
        contract_last = (((1,), (1,)), ((), ()))
        two = lax.dot_general(g2[...], cath[...], contract_last, preferred_element_type=F32)
        one = lax.dot_general(g2[0:C, :], catl[...], contract_last, preferred_element_type=F32)
        total = two[0:C] + two[C:] + one

        @pl.when(core == 0)
        def _():
            mine[n] = total[0:32]
            theirs[n] = total[32:64]

        @pl.when(core == 1)
        def _():
            mine[n] = total[32:64]
            theirs[n] = total[0:32]

    def pass_on(n):
        core_copy(n).wait_recv()
        both = mine[n] + given[n]
        for e in range(2):
            m = 2 * n + e
            summed[m] = both[:, e * 128 : e * 128 + 128]
            pl.when(xy != m)(lambda m=m: xy_copy(m, xy, m).start())

    compute(0)
    pl.semaphore_wait(barrier, 8 + 1 + PLANE - 1 + DEEP - 1)
    core_copy(0).start()
    halo = []
    for r, (dx, dy) in enumerate(OFFSETS):
        copy = send(
            ge.at[pl.ds(TILES + r * HALO, HALO)],
            back.at[pl.ds(r * HALO, HALO)],
            halo_s.at[r],
            halo_r.at[r],
            beside(gx, gy, dx, dy),
        )
        copy.start()
        halo.append(copy)

    def stage(n, carry):
        compute(n)
        core_copy(n).start()
        pass_on(n - 1)
        return carry

    lax.fori_loop(1, NB // 2, stage, 0)
    pass_on(NB // 2 - 1)

    reducer = xy < NB
    own = jnp.minimum(xy, NB - 1)

    @pl.when(reducer)
    def _():
        xy_in[xy] = summed[own]
        for u in range(PLANE):
            pl.when(xy != u)(lambda u=u: xy_copy(0, u, 0).wait_recv())
        acc = xy_in[0]
        for u in range(1, PLANE):
            acc = acc + xy_in[u]
        z_in[z] = acc
        for d in range(1, DEEP):
            z_copy(d, z).start()
        for d in range(1, DEEP):
            z_copy(d, lax.rem(z + d, DEEP)).wait_recv()
        acc = z_in[0]
        for d in range(1, DEEP):
            acc = acc + z_in[d]
        half[own] = acc
        for u in range(PLANE):
            pl.when(xy != u)(lambda u=u: spread_copy(own, u).start())

    for m in range(NB):
        pl.when(xy != m)(lambda m=m: spread_copy(m, 0).wait_recv())
    end = send(half, out.at[core], end_s, end_r, other)
    end.start()
    out[core] = half[...]
    for n in range(NB // 2):
        core_copy(n).wait_send()
    for m in range(NB):
        pl.when(xy != m)(lambda m=m: xy_copy(m, xy, m).wait_send())

    @pl.when(reducer)
    def _():
        for d in range(1, DEEP):
            z_copy(d, z).wait_send()
        for u in range(PLANE):
            pl.when(xy != u)(lambda u=u: spread_copy(own, u).wait_send())

    for copy in halo:
        copy.wait()
    end.wait()


def finish_kernel(sends, ge, back, summed, gf, gwo):
    gx, gy = position()
    gf[...] = ge[...]
    for r, (dx, dy) in enumerate(OFFSETS):
        there = inside(gx, gy, -dx, -dy)
        for h in range(HALO):
            gf[sends[0, 0, r, h]] += back[r * HALO + h] * there
    for c in range(2):
        for m in range(NB):
            block = summed[c, m]
            gwo[2 * m, c * 32 : c * 32 + 32, :] = block[:, 0:C]
            if 2 * m + 1 < OFFS:
                gwo[2 * m + 1, c * 32 : c * 32 + 32, :] = block[:, C : 2 * C]


def shaped(shape, dtype=F32):
    return jax.ShapeDtypeStruct(shape, dtype)


def run_tiles(kernel_map, counts, xh, xl, wcat, wback, cotangent):
    return pl.pallas_call(
        tile_kernel,
        out_shape=(shaped((TILES, C, V)), shaped((WIDE, C, V)), shaped((2 * C, TILES * V), BF16)),
        in_specs=[SMEM, SMEM] + [VMEM] * 5,
        out_specs=(VMEM,) * 3,
        scratch_shapes=[
            pltpu.VMEM((PAIRS, KC, 2 * V), BF16),
            pltpu.VMEM((PAIRS, KC, 2 * V), BF16),
        ],
        compiler_params=pltpu.CompilerParams(vmem_limit_bytes=32 << 20),
    )(kernel_map, counts, xh, xl, wcat, wback, cotangent)


def per_device(features, weights, kernel_map, send_lists, counts, cotangent):
    dma = pltpu.SemaphoreType.DMA
    xh, xl, wcat, wback = pl.pallas_call(
        fetch_kernel,
        out_shape=(
            shaped((WIDE, C, V), BF16),
            shaped((WIDE, C, V), BF16),
            shaped((2 * C, KC), BF16),
            shaped((KC, 4 * C), BF16),
        ),
        in_specs=[SMEM, ANY, ANY],
        out_specs=(VMEM,) * 4,
        scratch_shapes=[
            pltpu.VMEM((TILES, C, V), F32),
            pltpu.VMEM((OFFS, C, C), F32),
            pltpu.VMEM((8 * HALO, C, V), F32),
            pltpu.VMEM((8 * HALO, C, V), F32),
            dma((2,)),
            dma((8,)),
            dma((8,)),
        ],
        compiler_params=pltpu.CompilerParams(collective_id=0, has_side_effects=True, vmem_limit_bytes=24 << 20),
    )(send_lists, features, weights)
    act, ge, g2 = run_tiles(kernel_map, counts, xh, xl, wcat, wback, cotangent)
    back, summed = pl.pallas_call(
        return_kernel,
        out_shape=(shaped((8 * HALO, C, V)), shaped((2, NB, 32, 128))),
        in_specs=[SMEM, VMEM, VMEM, VMEM, ANY],
        out_specs=(ANY, VMEM),
        scratch_shapes=[
            pltpu.VMEM((4 * C, TILES * V), BF16),
            pltpu.VMEM((4 * C, TILES * V), BF16),
            pltpu.VMEM((NB // 2, 32, 256), F32),
            pltpu.VMEM((NB // 2, 32, 256), F32),
            pltpu.VMEM((NB // 2, 32, 256), F32),
            pltpu.VMEM((NB, 32, 128), F32),
            pltpu.VMEM((PLANE, 32, 128), F32),
            pltpu.VMEM((DEEP, 32, 128), F32),
            pltpu.VMEM((NB, 32, 128), F32),
            dma((8,)),
            dma((8,)),
            dma((NB // 2,)),
            dma((NB // 2,)),
            dma((NB,)),
            dma((PLANE,)),
            dma((DEEP,)),
            dma((DEEP,)),
            dma((PLANE,)),
            dma((NB,)),
            dma,
            dma,
        ],
        compiler_params=pltpu.CompilerParams(collective_id=1, has_side_effects=True, vmem_limit_bytes=24 << 20),
    )(kernel_map, xh, xl, g2, ge)
    gf, gwo = pl.pallas_call(
        finish_kernel,
        out_shape=(shaped((TILES, C, V)), shaped((OFFS, C, C))),
        grid=(1,),
        in_specs=[SMEM, pl.BlockSpec((TILES, C, V), lambda i: (0, 0, 0)), VMEM, VMEM],
        out_specs=(VMEM, VMEM),
        compiler_params=pltpu.CompilerParams(vmem_limit_bytes=24 << 20),
    )(send_lists, ge, back, summed)
    return act[None, None], gf[None, None], gwo


def solution(mesh):
    placed = (
        P("gx", "gy", None, None, None),
        P(),
        P("gx", "gy", None, None),
        P("gx", "gy", None, None),
        P("gx", "gy"),
        P("gx", "gy", None, None, None),
    )
    return jax.shard_map(
        per_device,
        mesh=mesh,
        in_specs=placed,
        out_specs=(P("gx", "gy", None, None, None), P("gx", "gy", None, None, None), P()),
        check_vma=False,
    )
```

```python
import jax
import jax.numpy as jnp
from jax import lax
from jax.experimental import pallas as pl
from jax.experimental.pallas import tpu as pltpu
from jax.sharding import PartitionSpec as P

OFFSETS = ((-1, -1), (-1, 0), (-1, 1), (0, -1), (0, 1), (1, -1), (1, 0), (1, 1))
NX, NY = 32, 8
TILES, HALO, OFFS, C, V = 24, 4, 27, 64, 128
WIDE = TILES + 8 * HALO + 1
KC = 28 * C
NB = KC // 128
PLANE, DEEP = 16, 8
QUAD = 4
ENTRIES = TILES * OFFS
RANKS = 768
MESH = pl.DeviceIdType.MESH
F32, BF16 = jnp.float32, jnp.bfloat16
VMEM = pl.BlockSpec(memory_space=pltpu.VMEM)
ANY = pl.BlockSpec(memory_space=pl.ANY)
SMEM = pl.BlockSpec(memory_space=pltpu.SMEM)


def position():
    return lax.axis_index("gx"), lax.axis_index("gy")


def beside(gx, gy, dx, dy):
    return lax.rem(gx + (dx + NX), NX), lax.rem(gy + (dy + NY), NY)


def inside(gx, gy, dx, dy):
    ok = (gx + dx >= 0) & (gx + dx < NX) & (gy + dy >= 0) & (gy + dy < NY)
    return jnp.where(ok, 1.0, 0.0).astype(F32)


def halves(value):
    high = value.astype(BF16)
    return high, (value - high.astype(F32)).astype(BF16)


def main_kernel(
    kmap,
    sends,
    counts,
    kmap_rows,
    feat_hbm,
    weights_hbm,
    cot_hbm,
    act,
    ge,
    back,
    out,
    feat,
    weights,
    cot,
    xh,
    xl,
    wcat,
    wback,
    box,
    inbox,
    catch,
    catl,
    total,
    stacked,
    parts,
    runs,
    order_v,
    upto_v,
    order,
    upto,
    mine,
    theirs,
    given,
    summed,
    xy_in,
    z_in,
    half,
    load_sem,
    table_sem,
    in_s,
    in_r,
    halo_s,
    halo_r,
    core_s,
    core_r,
    xy_s,
    xy_r,
    z_s,
    z_r,
    spread_s,
    spread_r,
    end_s,
    end_r,
):
    gx, gy = position()
    core, z = lax.rem(gx, 2), gx // 4
    xy = (lax.rem(gx // 2, 2) * 2 + gy // 4) * 4 + lax.rem(gy, 4)

    def xy_device(u):
        return (z * 4 + (u // 8) * 2 + core, lax.rem(u // 4, 2) * 4 + lax.rem(u, 4))

    def z_device(d):
        return (lax.rem(z + d, DEEP) * 4 + lax.rem(gx, 4), gy)

    other = (gx + 1 - 2 * core, gy)
    load_feat = pltpu.make_async_copy(feat_hbm.at[0, 0], feat, load_sem.at[0])
    load_weights = pltpu.make_async_copy(weights_hbm, weights, load_sem.at[1])
    load_cot = pltpu.make_async_copy(cot_hbm.at[0, 0], cot, load_sem.at[2])
    load_feat.start()
    load_weights.start()
    load_cot.start()
    barrier = pltpu.get_barrier_semaphore()

    def greet(device):
        pl.semaphore_signal(barrier, inc=1, device_id=device, device_id_type=MESH)

    for d in range(1, DEEP):
        greet(z_device(d))
    for dx, dy in OFFSETS:
        greet(beside(gx, gy, dx, dy))
    for u in range(PLANE):
        pl.when(xy != u)(lambda u=u: greet(xy_device(u)))
    greet(other)

    def send(src, dst, send_sem, recv_sem, device):
        return pltpu.make_async_remote_copy(
            src_ref=src, dst_ref=dst, send_sem=send_sem, recv_sem=recv_sem, device_id=device, device_id_type=MESH
        )

    load_feat.wait()
    for r in range(8):
        for h in range(HALO):
            box[r * HALO + h] = feat[sends[0, 0, r, h]]
    load_weights.wait()
    for m in range(NB):
        left = weights[2 * m]
        right = weights[2 * m + 1] if 2 * m + 1 < OFFS else jnp.zeros((C, C), F32)
        pair = jnp.concatenate([left, right], axis=1)
        high, low = halves(pair)
        wcat[0:C, m * 128 : m * 128 + 128] = high
        wcat[C : 2 * C, m * 128 : m * 128 + 128] = low
        turned = pair.T
        high = turned.astype(BF16).astype(F32)
        both = jnp.concatenate([high, turned - high], axis=1).astype(BF16)
        wback[m * 128 : m * 128 + 128, 0:128] = both
        wback[m * 128 : m * 128 + 128, 128:256] = both

    pl.semaphore_wait(barrier, 8 + 1 + PLANE - 1 + DEEP - 1)
    arriving = []
    for r, (dx, dy) in enumerate(OFFSETS):
        block = pl.ds(r * HALO, HALO)
        copy = send(box.at[block], inbox.at[block], in_s.at[r], in_r.at[r], beside(gx, gy, -dx, -dy))
        copy.start()
        arriving.append(copy)

    def split_tile(t, carry):
        xh[t], xl[t] = halves(feat[t])
        return carry

    lax.fori_loop(0, TILES, split_tile, 0)
    xh[WIDE - 1] = jnp.zeros((C, V), BF16)
    xl[WIDE - 1] = jnp.zeros((C, V), BF16)
    total[...] = jnp.zeros_like(total)
    catch[OFFS * C : KC, :] = jnp.zeros((C, QUAD * V), BF16)
    catl[OFFS * C : KC, :] = jnp.zeros((C, QUAD * V), BF16)

    place = lax.broadcasted_iota(jnp.int32, (TILES, OFFS), 0) * OFFS + lax.broadcasted_iota(jnp.int32, (TILES, OFFS), 1)
    keys = kmap_rows[0, 0] * 1024 + place
    lanes = lax.broadcasted_iota(jnp.int32, (8, 128), 1)

    def rank_row(t, carry):
        ranks, below = carry
        for k in range(OFFS):
            entry = kmap[0, 0, t, k]
            ranks = ranks + jnp.where(keys > entry * 1024 + (t * OFFS + k), 1, 0)
            below = below + jnp.where(lanes >= entry, 1, 0)
        return ranks, below

    ranks, below = lax.fori_loop(
        0, TILES, rank_row, (jnp.zeros((TILES, OFFS), jnp.int32), jnp.zeros((8, 128), jnp.int32))
    )
    upto_v[...] = below
    spots = lax.broadcasted_iota(jnp.int32, (TILES, RANKS), 1)
    found = jnp.zeros((TILES, RANKS), jnp.int32)
    for k in range(OFFS):
        found = found + jnp.where(ranks[:, k : k + 1] == spots, keys[:, k : k + 1], 0)
    order_v[...] = jnp.broadcast_to(jnp.sum(found, axis=0, keepdims=True), (8, RANKS))
    tables = [
        pltpu.make_async_copy(order_v, order, table_sem.at[0]),
        pltpu.make_async_copy(upto_v, upto, table_sem.at[1]),
    ]
    for table in tables:
        table.start()
    load_cot.wait()
    for r, (dx, dy) in enumerate(OFFSETS):
        arriving[r].wait_recv()
        there = inside(gx, gy, dx, dy)
        for h in range(HALO):
            slot = r * HALO + h
            xh[TILES + slot], xl[TILES + slot] = halves(inbox[slot] * there)
    for copy in arriving:
        copy.wait_send()
    for table in tables:
        table.wait()

    contract_last = (((1,), (1,)), ((), ()))

    def forward(p, carry):
        for k in range(OFFS):
            for h in range(QUAD):
                slot = kmap[0, 0, p * QUAD + h, k]
                catch[k * C : k * C + C, h * V : h * V + V] = xh[slot]
                catl[k * C : k * C + C, h * V : h * V + V] = xl[slot]
        first = jnp.dot(wcat[...], catch[...], preferred_element_type=F32)
        second = jnp.dot(wcat[0:C, :], catl[...], preferred_element_type=F32)
        pre = first[0:C] + first[C:] + second
        sig = jax.nn.sigmoid(pre)
        slope = sig * (1.0 + pre * (1.0 - sig))
        value = pre * sig
        grads = []
        for h in range(QUAD):
            tile = p * QUAD + h
            live = jnp.where(tile < counts[0, 0], 1.0, 0.0).astype(F32)
            act[tile] = value[:, h * V : h * V + V] * live
            grads.append(cot[tile] * live * slope[:, h * V : h * V + V])
        gh, gl = halves(jnp.concatenate(grads, axis=1))
        stacked[p, 0:C] = gh
        stacked[p, C : 2 * C] = gl
        two = lax.dot_general(
            jnp.concatenate([gh, gl], axis=0), catch[...], contract_last, preferred_element_type=F32
        )
        one = lax.dot_general(gh, catl[...], contract_last, preferred_element_type=F32)
        total[...] += two[0:C] + two[C:] + one
        return carry

    lax.fori_loop(0, TILES // QUAD, forward, 0)

    core_copy = send(theirs, given, core_s, core_r, other)

    def xy_copy(m, source, target):
        return send(summed.at[m], xy_in.at[source], xy_s.at[m], xy_r.at[source], xy_device(target))

    def z_copy(d, slot):
        return send(z_in.at[slot], z_in.at[slot], z_s.at[d], z_r.at[slot], z_device(d))

    def spread_copy(m, target):
        return send(half.at[m], half.at[m], spread_s.at[target], spread_r.at[m], xy_device(target))

    reducer = xy < NB
    own = jnp.minimum(xy, NB - 1)
    for c in range(2):

        @pl.when(core == c)
        def _(c=c):
            for m in range(NB):
                mine[m] = total[c * 32 : c * 32 + 32, m * 128 : m * 128 + 128]
                theirs[m] = total[32 - c * 32 : 64 - c * 32, m * 128 : m * 128 + 128]

    core_copy.start()

    def backward(p, carry):
        gh = stacked[p, 0:C]
        gl = stacked[p, C : 2 * C]
        four = jnp.concatenate([gh, gh, gl, gl], axis=0)
        for k in range(OFFS):
            part = jnp.dot(wback[k * C : k * C + C, :], four, preferred_element_type=F32)
            for h in range(QUAD):
                parts[(p * QUAD + h) * OFFS + k] = part[:, h * V : h * V + V]
        return carry

    lax.fori_loop(0, 2, backward, 0)
    core_copy.wait_recv()
    for m in range(NB):
        summed[m] = mine[m] + given[m]
    for m in range(NB):
        pl.when(xy != m)(lambda m=m: xy_copy(m, xy, m).start())
    lax.fori_loop(2, TILES // QUAD, backward, 0)

    @pl.when(reducer)
    def _():
        xy_in[xy] = summed[own]
        for u in range(PLANE):
            pl.when(xy != u)(lambda u=u: xy_copy(0, u, 0).wait_recv())
        acc = xy_in[0]
        for u in range(1, PLANE):
            acc = acc + xy_in[u]
        z_in[z] = acc
        for d in range(1, DEEP):
            z_copy(d, z).start()

    def scan(step, carry):
        acc, last = carry
        for i in range(8):
            spot = step * 8 + i
            key = order[0, spot]
            entry = lax.shift_right_logical(key, 10)
            same = jnp.where(entry == last, 1.0, 0.0).astype(F32)
            acc = acc * same + parts[lax.bitwise_and(key, 1023)]
            runs[spot] = acc
            last = entry
        return acc, last

    lax.fori_loop(0, ENTRIES // 8, scan, (jnp.zeros((C, V), F32), jnp.int32(WIDE)))

    def gathered(entry):
        stop = upto[0, entry]
        begin = upto[0, entry - 1] if entry > 0 else jnp.int32(0)
        return runs[jnp.maximum(stop - 1, 0)] * jnp.where(stop > begin, 1.0, 0.0).astype(F32)

    leaving = []
    for r, (dx, dy) in enumerate(OFFSETS):
        for h in range(HALO):
            box[r * HALO + h] = gathered(TILES + r * HALO + h)
        block = pl.ds(r * HALO, HALO)
        copy = send(box.at[block], back.at[block], halo_s.at[r], halo_r.at[r], beside(gx, gy, dx, dy))
        copy.start()
        leaving.append(copy)

    @pl.when(reducer)
    def _():
        for d in range(1, DEEP):
            z_copy(d, lax.rem(z + d, DEEP)).wait_recv()
        acc = z_in[0]
        for d in range(1, DEEP):
            acc = acc + z_in[d]
        half[own] = acc
        for u in range(PLANE):
            pl.when(xy != u)(lambda u=u: spread_copy(own, u).start())

    for t in range(TILES):
        ge[t] = gathered(t)
    for m in range(NB):
        pl.when(xy != m)(lambda m=m: spread_copy(m, 0).wait_recv())
    end = send(half, out.at[core], end_s, end_r, other)
    end.start()
    out[core] = half[...]
    core_copy.wait_send()
    for m in range(NB):
        pl.when(xy != m)(lambda m=m: xy_copy(m, xy, m).wait_send())

    @pl.when(reducer)
    def _():
        for d in range(1, DEEP):
            z_copy(d, z).wait_send()
        for u in range(PLANE):
            pl.when(xy != u)(lambda u=u: spread_copy(own, u).wait_send())

    for copy in leaving:
        copy.wait()
    end.wait()


def finish_kernel(sends, ge, back, summed, act, acts, gf, gwo):
    gx, gy = position()
    acts[...] = act[...]
    gf[...] = ge[...]
    for r, (dx, dy) in enumerate(OFFSETS):
        there = inside(gx, gy, -dx, -dy)
        for h in range(HALO):
            gf[sends[0, 0, r, h]] += back[r * HALO + h] * there
    for c in range(2):
        for m in range(NB):
            block = summed[c, m]
            gwo[2 * m, c * 32 : c * 32 + 32, :] = block[:, 0:C]
            if 2 * m + 1 < OFFS:
                gwo[2 * m + 1, c * 32 : c * 32 + 32, :] = block[:, C : 2 * C]


def shaped(shape, dtype=F32):
    return jax.ShapeDtypeStruct(shape, dtype)


def per_device(features, weights, kernel_map, send_lists, counts, cotangent):
    dma = pltpu.SemaphoreType.DMA
    vmem = pltpu.VMEM
    act, ge, back, summed = pl.pallas_call(
        main_kernel,
        out_shape=(
            shaped((TILES, C, V)),
            shaped((TILES, C, V)),
            shaped((8 * HALO, C, V)),
            shaped((2, NB, 32, 128)),
        ),
        in_specs=[SMEM, SMEM, SMEM, VMEM, ANY, ANY, ANY],
        out_specs=(VMEM, VMEM, ANY, VMEM),
        scratch_shapes=[
            vmem((TILES, C, V), F32),
            vmem((OFFS, C, C), F32),
            vmem((TILES, C, V), F32),
            vmem((WIDE, C, V), BF16),
            vmem((WIDE, C, V), BF16),
            vmem((2 * C, KC), BF16),
            vmem((KC, 4 * C), BF16),
            vmem((8 * HALO, C, V), F32),
            vmem((8 * HALO, C, V), F32),
            vmem((KC, QUAD * V), BF16),
            vmem((KC, QUAD * V), BF16),
            vmem((C, KC), F32),
            vmem((TILES // QUAD, 2 * C, QUAD * V), BF16),
            vmem((ENTRIES, C, V), F32),
            vmem((ENTRIES, C, V), F32),
            vmem((8, RANKS), jnp.int32),
            vmem((8, 128), jnp.int32),
            pltpu.SMEM((8, RANKS), jnp.int32),
            pltpu.SMEM((8, 128), jnp.int32),
            vmem((NB, 32, 128), F32),
            vmem((NB, 32, 128), F32),
            vmem((NB, 32, 128), F32),
            vmem((NB, 32, 128), F32),
            vmem((PLANE, 32, 128), F32),
            vmem((DEEP, 32, 128), F32),
            vmem((NB, 32, 128), F32),
            dma((3,)),
            dma((2,)),
            dma((8,)),
            dma((8,)),
            dma((8,)),
            dma((8,)),
            dma,
            dma,
            dma((NB,)),
            dma((PLANE,)),
            dma((DEEP,)),
            dma((DEEP,)),
            dma((PLANE,)),
            dma((NB,)),
            dma,
            dma,
        ],
        compiler_params=pltpu.CompilerParams(collective_id=0, has_side_effects=True, vmem_limit_bytes=60 << 20),
    )(kernel_map, send_lists, counts, kernel_map, features, weights, cotangent)
    act, gf, gwo = pl.pallas_call(
        finish_kernel,
        out_shape=(shaped((TILES, C, V)), shaped((TILES, C, V)), shaped((OFFS, C, C))),
        in_specs=[SMEM, VMEM, VMEM, VMEM, VMEM],
        out_specs=(VMEM, VMEM, VMEM),
        compiler_params=pltpu.CompilerParams(vmem_limit_bytes=24 << 20),
    )(send_lists, ge, back, summed, act)
    return act[None, None], gf[None, None], gwo


def solution(mesh):
    placed = (
        P("gx", "gy", None, None, None),
        P(),
        P("gx", "gy", None, None),
        P("gx", "gy", None, None),
        P("gx", "gy"),
        P("gx", "gy", None, None, None),
    )
    return jax.shard_map(
        per_device,
        mesh=mesh,
        in_specs=placed,
        out_specs=(P("gx", "gy", None, None, None), P("gx", "gy", None, None, None), P()),
        check_vma=False,
    )
```

```python
import jax
import jax.numpy as jnp
from jax import lax
from jax.experimental import pallas as pl
from jax.experimental.pallas import tpu as pltpu
from jax.sharding import PartitionSpec as P

OFFSETS = ((-1, -1), (-1, 0), (-1, 1), (0, -1), (0, 1), (1, -1), (1, 0), (1, 1))
NX, NY = 32, 8
TILES, HALO, OFFS, C, V = 24, 4, 27, 64, 128
WIDE = TILES + 8 * HALO + 1
KC = 28 * C
NB = KC // 128
PLANE, DEEP = 16, 8
QUAD = 4
ENTRIES = TILES * OFFS
RANKS = 768
PIECE = 56
MESH = pl.DeviceIdType.MESH
F32, BF16 = jnp.float32, jnp.bfloat16
VMEM = pl.BlockSpec(memory_space=pltpu.VMEM)
ANY = pl.BlockSpec(memory_space=pl.ANY)
SMEM = pl.BlockSpec(memory_space=pltpu.SMEM)


def position():
    return lax.axis_index("gx"), lax.axis_index("gy")


def beside(gx, gy, dx, dy):
    return lax.rem(gx + (dx + NX), NX), lax.rem(gy + (dy + NY), NY)


def inside(gx, gy, dx, dy):
    ok = (gx + dx >= 0) & (gx + dx < NX) & (gy + dy >= 0) & (gy + dy < NY)
    return jnp.where(ok, 1.0, 0.0).astype(F32)


def halves(value):
    high = value.astype(BF16)
    return high, (value - high.astype(F32)).astype(BF16)


def main_kernel(
    kmap,
    sends,
    counts,
    kmap_rows,
    feat_hbm,
    weights_hbm,
    cot_hbm,
    act_hbm,
    ge_hbm,
    back,
    out,
    feat,
    weights,
    cot,
    xh,
    xl,
    wcat,
    wback,
    box,
    inbox,
    catch,
    catl,
    total,
    stacked,
    parts,
    runs,
    order_v,
    upto_v,
    order,
    upto,
    mine,
    theirs,
    given,
    summed,
    xy_in,
    z_in,
    half,
    load_sem,
    store_sem,
    table_sem,
    in_s,
    in_r,
    halo_s,
    halo_r,
    core_s,
    core_r,
    xy_s,
    xy_r,
    fold_s,
    fold_r,
    spread_s,
    spread_r,
    end_s,
    end_r,
):
    gx, gy = position()
    core, z = lax.rem(gx, 2), gx // 4
    xy = (lax.rem(gx // 2, 2) * 2 + gy // 4) * 4 + lax.rem(gy, 4)

    def xy_device(u):
        return (z * 4 + (u // 8) * 2 + core, lax.rem(u // 4, 2) * 4 + lax.rem(u, 4))

    def z_device(d):
        return (lax.rem(z + d, DEEP) * 4 + lax.rem(gx, 4), gy)

    other = (gx + 1 - 2 * core, gy)
    load_feat = pltpu.make_async_copy(feat_hbm.at[0, 0], feat, load_sem.at[0])
    load_weights = pltpu.make_async_copy(weights_hbm, weights, load_sem.at[1])
    load_cot = pltpu.make_async_copy(cot_hbm.at[0, 0], cot, load_sem.at[2])
    load_feat.start()
    load_weights.start()
    load_cot.start()
    barrier = pltpu.get_barrier_semaphore()

    def greet(device):
        pl.semaphore_signal(barrier, inc=1, device_id=device, device_id_type=MESH)

    for d in range(1, DEEP):
        greet(z_device(d))
    for dx, dy in OFFSETS:
        greet(beside(gx, gy, dx, dy))
    for u in range(PLANE):
        pl.when(xy != u)(lambda u=u: greet(xy_device(u)))
    greet(other)

    def send(src, dst, send_sem, recv_sem, device):
        return pltpu.make_async_remote_copy(
            src_ref=src, dst_ref=dst, send_sem=send_sem, recv_sem=recv_sem, device_id=device, device_id_type=MESH
        )

    load_feat.wait()
    for r in range(8):
        for h in range(HALO):
            box[r * HALO + h] = feat[sends[0, 0, h, r]]
    pl.semaphore_wait(barrier, 8 + 1 + PLANE - 1 + DEEP - 1)
    arriving = []
    for r, (dx, dy) in enumerate(OFFSETS):
        block = pl.ds(r * HALO, HALO)
        copy = send(box.at[block], inbox.at[block], in_s.at[r], in_r.at[r], beside(gx, gy, -dx, -dy))
        copy.start()
        arriving.append(copy)

    load_weights.wait()
    for m in range(NB):
        left = weights[2 * m]
        right = weights[2 * m + 1] if 2 * m + 1 < OFFS else jnp.zeros((C, C), F32)
        pair = jnp.concatenate([left, right], axis=1)
        high, low = halves(pair)
        wcat[0:C, m * 128 : m * 128 + 128] = high
        wcat[C : 2 * C, m * 128 : m * 128 + 128] = low
        turned = pair.T
        high = turned.astype(BF16).astype(F32)
        both = jnp.concatenate([high, turned - high], axis=1).astype(BF16)
        wback[m * 128 : m * 128 + 128, 0:128] = both
        wback[m * 128 : m * 128 + 128, 128:256] = both

    def split_tile(t, carry):
        xh[t], xl[t] = halves(feat[t])
        return carry

    lax.fori_loop(0, TILES, split_tile, 0)
    xh[WIDE - 1] = jnp.zeros((C, V), BF16)
    xl[WIDE - 1] = jnp.zeros((C, V), BF16)
    total[...] = jnp.zeros_like(total)
    catch[OFFS * C : KC, :] = jnp.zeros((C, QUAD * V), BF16)
    catl[OFFS * C : KC, :] = jnp.zeros((C, QUAD * V), BF16)

    place = lax.broadcasted_iota(jnp.int32, (TILES, OFFS), 0) * OFFS + lax.broadcasted_iota(jnp.int32, (TILES, OFFS), 1)
    keys = kmap_rows[0, 0] * 1024 + place
    lanes = lax.broadcasted_iota(jnp.int32, (8, 128), 1)

    def rank_row(t, carry):
        ranks, below = carry
        for k in range(OFFS):
            entry = kmap[0, 0, t, k]
            ranks = ranks + jnp.where(keys > entry * 1024 + (t * OFFS + k), 1, 0)
            below = below + jnp.where(lanes >= entry, 1, 0)
        return ranks, below

    ranks, below = lax.fori_loop(
        0, TILES, rank_row, (jnp.zeros((TILES, OFFS), jnp.int32), jnp.zeros((8, 128), jnp.int32))
    )
    upto_v[...] = below
    spots = lax.broadcasted_iota(jnp.int32, (TILES, RANKS), 1)
    found = jnp.zeros((TILES, RANKS), jnp.int32)
    for k in range(OFFS):
        found = found + jnp.where(ranks[:, k : k + 1] == spots, keys[:, k : k + 1], 0)
    order_v[...] = jnp.broadcast_to(jnp.sum(found, axis=0, keepdims=True), (8, RANKS))
    tables = [
        pltpu.make_async_copy(order_v, order, table_sem.at[0]),
        pltpu.make_async_copy(upto_v, upto, table_sem.at[1]),
    ]
    for table in tables:
        table.start()
    load_cot.wait()
    for r, (dx, dy) in enumerate(OFFSETS):
        arriving[r].wait_recv()
        there = inside(gx, gy, dx, dy)
        for h in range(HALO):
            slot = r * HALO + h
            xh[TILES + slot], xl[TILES + slot] = halves(inbox[slot] * there)
    for copy in arriving:
        copy.wait_send()
    for table in tables:
        table.wait()

    contract_last = (((1,), (1,)), ((), ()))

    def forward(p, carry):
        for k in range(OFFS):
            for h in range(QUAD):
                slot = kmap[0, 0, p * QUAD + h, k]
                catch[k * C : k * C + C, h * V : h * V + V] = xh[slot]
                catl[k * C : k * C + C, h * V : h * V + V] = xl[slot]
        first = jnp.dot(wcat[...], catch[...], preferred_element_type=F32)
        second = jnp.dot(wcat[0:C, :], catl[...], preferred_element_type=F32)
        pre = first[0:C] + first[C:] + second
        sig = jax.nn.sigmoid(pre)
        slope = sig * (1.0 + pre * (1.0 - sig))
        value = pre * sig
        grads = []
        for h in range(QUAD):
            tile = p * QUAD + h
            live = jnp.where(tile < counts[0, 0], 1.0, 0.0).astype(F32)
            feat[tile] = value[:, h * V : h * V + V] * live
            grads.append(cot[tile] * live * slope[:, h * V : h * V + V])
        gh, gl = halves(jnp.concatenate(grads, axis=1))
        stacked[p, 0:C] = gh
        stacked[p, C : 2 * C] = gl
        two = lax.dot_general(
            jnp.concatenate([gh, gl], axis=0), catch[...], contract_last, preferred_element_type=F32
        )
        one = lax.dot_general(gh, catl[...], contract_last, preferred_element_type=F32)
        total[...] += two[0:C] + two[C:] + one
        return carry

    lax.fori_loop(0, TILES // QUAD, forward, 0)

    store_act = pltpu.make_async_copy(feat, act_hbm, store_sem.at[0])
    store_act.start()
    core_copy = send(theirs, given, core_s, core_r, other)

    def fold_copy(d, target, source):
        return send(summed.at[target], z_in.at[source], fold_s.at[d], fold_r.at[source], z_device(d))

    def plane_copy(u, source):
        return send(xy_in.at[source], xy_in.at[source], xy_s.at[u], xy_r.at[source], xy_device(u))

    def spread_copy(d, source):
        return send(half.at[source], half.at[source], spread_s.at[d], spread_r.at[source], z_device(d))

    def others(act):
        for u in range(PLANE):
            pl.when(xy != u)(lambda u=u: act(u))

    def tree(values):
        while len(values) > 1:
            values = [values[i] + values[i + 1] for i in range(0, len(values) - 1, 2)] + values[len(values) & ~1 :]
        return values[0]

    for c in range(2):

        @pl.when(core == c)
        def _(c=c):
            for i in range(DEEP * PIECE // 8):
                m, row = i // 4, (i % 4) * 8
                mine[i // 7, (i % 7) * 8 : (i % 7) * 8 + 8] = total[c * 32 + row : c * 32 + row + 8, m * 128 : m * 128 + 128]
                row += 32 - c * 32
                theirs[i // 7, (i % 7) * 8 : (i % 7) * 8 + 8] = total[row : row + 8, m * 128 : m * 128 + 128]

    core_copy.start()

    def backward(p, carry):
        gh = stacked[p, 0:C]
        gl = stacked[p, C : 2 * C]
        four = jnp.concatenate([gh, gh, gl, gl], axis=0)
        for k in range(OFFS):
            part = jnp.dot(wback[k * C : k * C + C, :], four, preferred_element_type=F32)
            for h in range(QUAD):
                parts[(p * QUAD + h) * OFFS + k] = part[:, h * V : h * V + V]
        return carry

    lax.fori_loop(0, 2, backward, 0)
    core_copy.wait_recv()
    summed[...] = mine[...] + given[...]
    for d in range(1, DEEP):
        fold_copy(d, lax.rem(z + d, DEEP), z).start()
    z_in[z] = summed[z]
    lax.fori_loop(2, TILES // QUAD, backward, 0)

    for d in range(1, DEEP):
        fold_copy(d, 0, lax.rem(z + d, DEEP)).wait_recv()
    xy_in[xy] = tree([z_in[d] for d in range(DEEP)])
    others(lambda u: plane_copy(u, xy).start())

    def scan(step, carry):
        acc, last = carry
        for i in range(8):
            spot = step * 8 + i
            key = order[0, spot]
            entry = lax.shift_right_logical(key, 10)
            same = jnp.where(entry == last, 1.0, 0.0).astype(F32)
            acc = acc * same + parts[lax.bitwise_and(key, 1023)]
            runs[spot] = acc
            last = entry
        return acc, last

    lax.fori_loop(0, ENTRIES // 8, scan, (jnp.zeros((C, V), F32), jnp.int32(WIDE)))

    def gathered(entry):
        stop = upto[0, entry]
        begin = upto[0, entry - 1] if entry > 0 else jnp.int32(0)
        return runs[jnp.maximum(stop - 1, 0)] * jnp.where(stop > begin, 1.0, 0.0).astype(F32)

    leaving = []
    for r, (dx, dy) in enumerate(OFFSETS):
        for h in range(HALO):
            box[r * HALO + h] = gathered(TILES + r * HALO + h)
        block = pl.ds(r * HALO, HALO)
        copy = send(box.at[block], back.at[block], halo_s.at[r], halo_r.at[r], beside(gx, gy, dx, dy))
        copy.start()
        leaving.append(copy)

    for t in range(TILES):
        cot[t] = gathered(t)
    store_ge = pltpu.make_async_copy(cot, ge_hbm, store_sem.at[1])
    store_ge.start()
    others(lambda u: plane_copy(u, u).wait_recv())
    half[z] = tree([xy_in[u] for u in range(PLANE)])
    for d in range(1, DEEP):
        spread_copy(d, z).start()
    for d in range(1, DEEP):
        spread_copy(d, lax.rem(z + d, DEEP)).wait_recv()
    end = send(half, out.at[core], end_s, end_r, other)
    end.start()
    store_half = pltpu.make_async_copy(half, out.at[core], store_sem.at[2])
    store_half.start()
    core_copy.wait_send()
    for d in range(1, DEEP):
        fold_copy(d, 0, z).wait_send()
        spread_copy(d, z).wait_send()
    others(lambda u: plane_copy(u, xy).wait_send())
    store_act.wait()
    store_ge.wait()
    store_half.wait()
    for copy in leaving:
        copy.wait()
    end.wait()


def finish_kernel(sends, ge_hbm, back_hbm, summed_hbm, act_hbm, acts_hbm, gf, gwo, back, summed, sem):
    gx, gy = position()
    load_sums = pltpu.make_async_copy(summed_hbm, summed, sem.at[0])
    load_ge = pltpu.make_async_copy(ge_hbm, gf, sem.at[1])
    load_back = pltpu.make_async_copy(back_hbm, back, sem.at[2])
    move_act = pltpu.make_async_copy(act_hbm, acts_hbm, sem.at[3])
    for copy in (load_sums, load_ge, load_back, move_act):
        copy.start()
    load_sums.wait()
    for c in range(2):
        for i in range(DEEP * PIECE // 8):
            m, row = i // 4, c * 32 + (i % 4) * 8
            block = summed[c, i // 7, (i % 7) * 8 : (i % 7) * 8 + 8]
            gwo[2 * m, row : row + 8, :] = block[:, 0:C]
            if 2 * m + 1 < OFFS:
                gwo[2 * m + 1, row : row + 8, :] = block[:, C : 2 * C]
    load_ge.wait()
    load_back.wait()
    for r, (dx, dy) in enumerate(OFFSETS):
        there = inside(gx, gy, -dx, -dy)
        for h in range(HALO):
            gf[sends[0, 0, h, r]] += back[r * HALO + h] * there
    move_act.wait()


def shaped(shape, dtype=F32):
    return jax.ShapeDtypeStruct(shape, dtype)


def per_device(features, weights, kernel_map, send_lists, counts, cotangent):
    send_lists = jnp.swapaxes(send_lists, 2, 3)
    dma = pltpu.SemaphoreType.DMA
    vmem = pltpu.VMEM
    act, ge, back, summed = pl.pallas_call(
        main_kernel,
        out_shape=(
            shaped((TILES, C, V)),
            shaped((TILES, C, V)),
            shaped((8 * HALO, C, V)),
            shaped((2, DEEP, PIECE, 128)),
        ),
        in_specs=[SMEM, SMEM, SMEM, VMEM, ANY, ANY, ANY],
        out_specs=(ANY, ANY, ANY, ANY),
        scratch_shapes=[
            vmem((TILES, C, V), F32),
            vmem((OFFS, C, C), F32),
            vmem((TILES, C, V), F32),
            vmem((WIDE, C, V), BF16),
            vmem((WIDE, C, V), BF16),
            vmem((2 * C, KC), BF16),
            vmem((KC, 4 * C), BF16),
            vmem((8 * HALO, C, V), F32),
            vmem((8 * HALO, C, V), F32),
            vmem((KC, QUAD * V), BF16),
            vmem((KC, QUAD * V), BF16),
            vmem((C, KC), F32),
            vmem((TILES // QUAD, 2 * C, QUAD * V), BF16),
            vmem((ENTRIES, C, V), F32),
            vmem((ENTRIES, C, V), F32),
            vmem((8, RANKS), jnp.int32),
            vmem((8, 128), jnp.int32),
            pltpu.SMEM((8, RANKS), jnp.int32),
            pltpu.SMEM((8, 128), jnp.int32),
            vmem((DEEP, PIECE, 128), F32),
            vmem((DEEP, PIECE, 128), F32),
            vmem((DEEP, PIECE, 128), F32),
            vmem((DEEP, PIECE, 128), F32),
            vmem((PLANE, PIECE, 128), F32),
            vmem((DEEP, PIECE, 128), F32),
            vmem((DEEP, PIECE, 128), F32),
            dma((3,)),
            dma((3,)),
            dma((2,)),
            dma((8,)),
            dma((8,)),
            dma((8,)),
            dma((8,)),
            dma,
            dma,
            dma((PLANE,)),
            dma((PLANE,)),
            dma((DEEP,)),
            dma((DEEP,)),
            dma((DEEP,)),
            dma((DEEP,)),
            dma,
            dma,
        ],
        compiler_params=pltpu.CompilerParams(collective_id=0, has_side_effects=True, vmem_limit_bytes=60 << 20),
    )(kernel_map, send_lists, counts, kernel_map, features, weights, cotangent)
    act, gf, gwo = pl.pallas_call(
        finish_kernel,
        out_shape=(shaped((TILES, C, V)), shaped((TILES, C, V)), shaped((OFFS, C, C))),
        in_specs=[SMEM, ANY, ANY, ANY, ANY],
        out_specs=(ANY, VMEM, VMEM),
        scratch_shapes=[
            vmem((8 * HALO, C, V), F32),
            vmem((2, DEEP, PIECE, 128), F32),
            dma((4,)),
        ],
        compiler_params=pltpu.CompilerParams(vmem_limit_bytes=60 << 20),
    )(send_lists, ge, back, summed, act)
    return act[None, None], gf[None, None], gwo


def solution(mesh):
    placed = (
        P("gx", "gy", None, None, None),
        P(),
        P("gx", "gy", None, None),
        P("gx", "gy", None, None),
        P("gx", "gy"),
        P("gx", "gy", None, None, None),
    )
    return jax.shard_map(
        per_device,
        mesh=mesh,
        in_specs=placed,
        out_specs=(P("gx", "gy", None, None, None), P("gx", "gy", None, None, None), P()),
        check_vma=False,
    )
```

```python
import jax
import jax.numpy as jnp
from jax import lax
from jax.experimental import pallas as pl
from jax.experimental.pallas import tpu as pltpu
from jax.sharding import PartitionSpec as P

OFFSETS = ((-1, -1), (-1, 0), (-1, 1), (0, -1), (0, 1), (1, -1), (1, 0), (1, 1))
NX, NY = 32, 8
TILES, HALO, OFFS, C, V = 24, 4, 27, 64, 128
WIDE = TILES + 8 * HALO + 1
KC = 28 * C
NB = KC // 128
PLANE, DEEP = 16, 8
QUAD = 4
EARLY = (0, 2, 5, 7)
LATE = (1, 3, 4, 6)
ENTRIES = TILES * OFFS
RANKS = 768
MESH = pl.DeviceIdType.MESH
F32, BF16 = jnp.float32, jnp.bfloat16
VMEM = pl.BlockSpec(memory_space=pltpu.VMEM)
ANY = pl.BlockSpec(memory_space=pl.ANY)
SMEM = pl.BlockSpec(memory_space=pltpu.SMEM)


def position():
    return lax.axis_index("gx"), lax.axis_index("gy")


def beside(gx, gy, dx, dy):
    return lax.rem(gx + (dx + NX), NX), lax.rem(gy + (dy + NY), NY)


def inside(gx, gy, dx, dy):
    ok = (gx + dx >= 0) & (gx + dx < NX) & (gy + dy >= 0) & (gy + dy < NY)
    return jnp.where(ok, 1.0, 0.0).astype(F32)


def halves(value):
    high = value.astype(BF16)
    return high, (value - high.astype(F32)).astype(BF16)


def main_kernel(
    kmap,
    sends,
    counts,
    kmap_rows,
    feat_hbm,
    weights_hbm,
    cot_hbm,
    act_hbm,
    ge_hbm,
    back,
    out,
    feat,
    weights,
    cot,
    xh,
    xl,
    wcat,
    wback,
    box,
    inbox,
    catch,
    catl,
    nexth,
    nextl,
    total,
    stacked,
    parts,
    runs,
    order_v,
    upto_v,
    order,
    upto,
    mine,
    theirs,
    given,
    summed,
    xy_in,
    z_in,
    half,
    load_sem,
    store_sem,
    table_sem,
    in_s,
    in_r,
    halo_s,
    halo_r,
    core_s,
    core_r,
    xy_s,
    xy_r,
    fold_s,
    fold_r,
    spread_s,
    spread_r,
    end_s,
    end_r,
):
    gx, gy = position()
    core, z = lax.rem(gx, 2), gx // 4
    xy = (lax.rem(gx // 2, 2) * 2 + gy // 4) * 4 + lax.rem(gy, 4)

    def xy_device(u):
        return (z * 4 + (u // 8) * 2 + core, lax.rem(u // 4, 2) * 4 + lax.rem(u, 4))

    def z_device(d):
        return (lax.rem(z + d, DEEP) * 4 + lax.rem(gx, 4), gy)

    other = (gx + 1 - 2 * core, gy)
    load_feat = pltpu.make_async_copy(feat_hbm.at[0, 0], feat, load_sem.at[0])
    load_weights = pltpu.make_async_copy(weights_hbm, weights, load_sem.at[1])
    load_cot = pltpu.make_async_copy(cot_hbm.at[0, 0], cot, load_sem.at[2])
    load_feat.start()
    load_weights.start()
    load_cot.start()
    barrier = pltpu.get_barrier_semaphore()

    def greet(device):
        pl.semaphore_signal(barrier, inc=1, device_id=device, device_id_type=MESH)

    for d in range(1, DEEP):
        greet(z_device(d))
    for dx, dy in OFFSETS:
        greet(beside(gx, gy, dx, dy))
    for u in range(PLANE):
        pl.when(xy != u)(lambda u=u: greet(xy_device(u)))
    greet(other)

    def send(src, dst, send_sem, recv_sem, device):
        return pltpu.make_async_remote_copy(
            src_ref=src, dst_ref=dst, send_sem=send_sem, recv_sem=recv_sem, device_id=device, device_id_type=MESH
        )

    load_feat.wait()
    for r in range(8):
        for h in range(HALO):
            box[r * HALO + h] = feat[sends[0, 0, h, r]]
    pl.semaphore_wait(barrier, 8 + 1 + PLANE - 1 + DEEP - 1)
    arriving = []
    for r, (dx, dy) in enumerate(OFFSETS):
        block = pl.ds(r * HALO, HALO)
        copy = send(box.at[block], inbox.at[block], in_s.at[r], in_r.at[r], beside(gx, gy, -dx, -dy))
        copy.start()
        arriving.append(copy)

    load_weights.wait()
    for m in range(NB):
        left = weights[2 * m]
        right = weights[2 * m + 1] if 2 * m + 1 < OFFS else jnp.zeros((C, C), F32)
        pair = jnp.concatenate([left, right], axis=1)
        high, low = halves(pair)
        wcat[0:C, m * 128 : m * 128 + 128] = high
        wcat[C : 2 * C, m * 128 : m * 128 + 128] = low
        turned = pair.T
        high = turned.astype(BF16).astype(F32)
        both = jnp.concatenate([high, turned - high], axis=1).astype(BF16)
        wback[m * 128 : m * 128 + 128, 0:128] = both
        wback[m * 128 : m * 128 + 128, 128:256] = both

    def split_tile(t, carry):
        xh[t], xl[t] = halves(feat[t])
        return carry

    lax.fori_loop(0, TILES, split_tile, 0)
    xh[WIDE - 1] = jnp.zeros((C, V), BF16)
    xl[WIDE - 1] = jnp.zeros((C, V), BF16)
    total[...] = jnp.zeros_like(total)
    for panel in (catch, catl, nexth, nextl):
        panel[OFFS * C : KC, :] = jnp.zeros((C, 2 * V), BF16)

    place = lax.broadcasted_iota(jnp.int32, (TILES, OFFS), 0) * OFFS + lax.broadcasted_iota(jnp.int32, (TILES, OFFS), 1)
    keys = kmap_rows[0, 0] * 1024 + place
    lanes = lax.broadcasted_iota(jnp.int32, (8, 128), 1)

    def rank_row(t, carry):
        ranks, below = carry
        for k in range(OFFS):
            entry = kmap[0, 0, t, k]
            ranks = ranks + jnp.where(keys > entry * 1024 + (t * OFFS + k), 1, 0)
            below = below + jnp.where(lanes >= entry, 1, 0)
        return ranks, below

    ranks, below = lax.fori_loop(
        0, TILES, rank_row, (jnp.zeros((TILES, OFFS), jnp.int32), jnp.zeros((8, 128), jnp.int32))
    )
    upto_v[...] = below
    spots = lax.broadcasted_iota(jnp.int32, (TILES, RANKS), 1)
    found = jnp.zeros((TILES, RANKS), jnp.int32)
    for k in range(OFFS):
        found = found + jnp.where(ranks[:, k : k + 1] == spots, keys[:, k : k + 1], 0)
    order_v[...] = jnp.broadcast_to(jnp.sum(found, axis=0, keepdims=True), (8, RANKS))
    tables = [
        pltpu.make_async_copy(order_v, order, table_sem.at[0]),
        pltpu.make_async_copy(upto_v, upto, table_sem.at[1]),
    ]
    for table in tables:
        table.start()
    load_cot.wait()
    for r, (dx, dy) in enumerate(OFFSETS):
        arriving[r].wait_recv()
        there = inside(gx, gy, dx, dy)
        for h in range(HALO):
            slot = r * HALO + h
            xh[TILES + slot], xl[TILES + slot] = halves(inbox[slot] * there)
    for copy in arriving:
        copy.wait_send()
    for table in tables:
        table.wait()

    contract_last = (((1,), (1,)), ((), ()))

    even, odd = (catch, catl), (nexth, nextl)
    pairs = TILES // 2

    def fill(p, panels):
        for k in range(OFFS):
            for h in range(2):
                slot = kmap[0, 0, p * 2 + h, k]
                panels[0][k * C : k * C + C, h * V : h * V + V] = xh[slot]
                panels[1][k * C : k * C + C, h * V : h * V + V] = xl[slot]

    def product(panels):
        first = jnp.dot(wcat[...], panels[0][...], preferred_element_type=F32)
        second = jnp.dot(wcat[0:C, :], panels[1][...], preferred_element_type=F32)
        return first[0:C] + first[C:] + second

    def activate(p, pre):
        sig = jax.nn.sigmoid(pre)
        slope = sig * (1.0 + pre * (1.0 - sig))
        value = pre * sig
        grads = []
        for h in range(2):
            tile = p * 2 + h
            live = jnp.where(tile < counts[0, 0], 1.0, 0.0).astype(F32)
            feat[tile] = value[:, h * V : h * V + V] * live
            grads.append(cot[tile] * live * slope[:, h * V : h * V + V])
        gh, gl = halves(jnp.concatenate(grads, axis=1))
        stacked[p, 0:C] = gh
        stacked[p, C : 2 * C] = gl

    def weigh(p, panels):
        two = lax.dot_general(stacked[p], panels[0][...], contract_last, preferred_element_type=F32)
        one = lax.dot_general(stacked[p, 0:C], panels[1][...], contract_last, preferred_element_type=F32)
        total[...] += two[0:C] + two[C:] + one

    def advance(p, panels, last):
        fill(p, panels)
        pre = product(panels)
        weigh(p - 1, last)
        activate(p, pre)

    def two_pairs(i, carry):
        advance(2 * i + 1, odd, even)
        advance(2 * i + 2, even, odd)
        return carry

    fill(0, even)
    activate(0, product(even))
    lax.fori_loop(0, pairs // 2 - 1, two_pairs, 0)
    advance(pairs - 1, odd, even)
    weigh(pairs - 1, odd)
    store_act = pltpu.make_async_copy(feat, act_hbm, store_sem.at[0])
    store_act.start()
    core_copy = send(theirs, given, core_s, core_r, other)

    def fold_copy(m, source):
        return send(summed.at[m], xy_in.at[source], xy_s.at[m], xy_r.at[source], xy_device(m))

    def z_copy(d, source):
        return send(z_in.at[source], z_in.at[source], fold_s.at[d], fold_r.at[source], z_device(d))

    def spread_copy(u, m):
        return send(half.at[m], half.at[m], spread_s.at[u], spread_r.at[m], xy_device(u))

    reducer = xy < NB
    own = jnp.minimum(xy, NB - 1)

    def pieces(act):
        for m in range(NB):
            pl.when(xy != m)(lambda m=m: act(m))

    def others(act):
        for u in range(PLANE):
            pl.when(xy != u)(lambda u=u: act(u))

    def tree(values):
        while len(values) > 1:
            values = [values[i] + values[i + 1] for i in range(0, len(values) - 1, 2)] + values[len(values) & ~1 :]
        return values[0]

    for c in range(2):

        @pl.when(core == c)
        def _(c=c):
            for m in range(NB):
                mine[m] = total[c * 32 : c * 32 + 32, m * 128 : m * 128 + 128]
                theirs[m] = total[32 - c * 32 : 64 - c * 32, m * 128 : m * 128 + 128]

    core_copy.start()

    def backward(p, carry):
        gh = jnp.concatenate([stacked[2 * p, 0:C], stacked[2 * p + 1, 0:C]], axis=1)
        gl = jnp.concatenate([stacked[2 * p, C : 2 * C], stacked[2 * p + 1, C : 2 * C]], axis=1)
        four = jnp.concatenate([gh, gh, gl, gl], axis=0)
        for k in range(OFFS):
            part = jnp.dot(wback[k * C : k * C + C, :], four, preferred_element_type=F32)
            for h in range(QUAD):
                parts[(p * QUAD + h) * OFFS + k] = part[:, h * V : h * V + V]
        return carry

    lax.fori_loop(0, 2, backward, 0)
    core_copy.wait_recv()
    summed[...] = mine[...] + given[...]
    pieces(lambda m: fold_copy(m, xy).start())
    xy_in[xy] = summed[own]
    lax.fori_loop(2, TILES // QUAD, backward, 0)

    @pl.when(reducer)
    def _():
        others(lambda u: fold_copy(0, u).wait_recv())
        z_in[z] = tree([xy_in[u] for u in range(PLANE)])
        for d in range(1, DEEP):
            z_copy(d, z).start()

    def scan(step, carry):
        acc, last = carry
        for i in range(8):
            spot = step * 8 + i
            key = order[0, spot]
            entry = lax.shift_right_logical(key, 10)
            same = jnp.where(entry == last, 1.0, 0.0).astype(F32)
            acc = acc * same + parts[lax.bitwise_and(key, 1023)]
            runs[spot] = acc
            last = entry
        return acc, last

    lax.fori_loop(0, ENTRIES // 8, scan, (jnp.zeros((C, V), F32), jnp.int32(WIDE)))

    def gathered(entry):
        stop = upto[0, entry]
        begin = upto[0, entry - 1] if entry > 0 else jnp.int32(0)
        return runs[jnp.maximum(stop - 1, 0)] * jnp.where(stop > begin, 1.0, 0.0).astype(F32)

    leaving = []

    def leave(r, dx, dy):
        for h in range(HALO):
            box[r * HALO + h] = gathered(TILES + r * HALO + h)
        block = pl.ds(r * HALO, HALO)
        copy = send(box.at[block], back.at[block], halo_s.at[r], halo_r.at[r], beside(gx, gy, dx, dy))
        copy.start()
        leaving.append(copy)

    for r in EARLY:
        leave(r, *OFFSETS[r])

    @pl.when(reducer)
    def _():
        for d in range(1, DEEP):
            z_copy(d, lax.rem(z + d, DEEP)).wait_recv()
        half[own] = tree([z_in[d] for d in range(DEEP)])
        others(lambda u: spread_copy(u, own).start())

    for r in LATE:
        leave(r, *OFFSETS[r])
    for t in range(TILES):
        cot[t] = gathered(t)
    store_ge = pltpu.make_async_copy(cot, ge_hbm, store_sem.at[1])
    store_ge.start()
    pieces(lambda m: spread_copy(0, m).wait_recv())
    end = send(half, out.at[core], end_s, end_r, other)
    end.start()
    store_half = pltpu.make_async_copy(half, out.at[core], store_sem.at[2])
    store_half.start()
    core_copy.wait_send()
    pieces(lambda m: fold_copy(m, xy).wait_send())

    @pl.when(reducer)
    def _():
        for d in range(1, DEEP):
            z_copy(d, z).wait_send()
        others(lambda u: spread_copy(u, own).wait_send())

    store_act.wait()
    store_ge.wait()
    store_half.wait()
    for copy in leaving:
        copy.wait()
    end.wait()


def finish_kernel(sends, ge_hbm, back_hbm, summed_hbm, act_hbm, acts, gf, gwo, back, summed, sem):
    gx, gy = position()
    load_sums = pltpu.make_async_copy(summed_hbm, summed, sem.at[0])
    load_ge = pltpu.make_async_copy(ge_hbm, gf, sem.at[1])
    load_back = pltpu.make_async_copy(back_hbm, back, sem.at[2])
    move_act = pltpu.make_async_copy(act_hbm, acts, sem.at[3])
    for copy in (load_sums, load_ge, load_back, move_act):
        copy.start()
    load_sums.wait()
    for c in range(2):
        for m in range(NB):
            block = summed[c, m]
            gwo[2 * m, c * 32 : c * 32 + 32, :] = block[:, 0:C]
            if 2 * m + 1 < OFFS:
                gwo[2 * m + 1, c * 32 : c * 32 + 32, :] = block[:, C : 2 * C]
    load_ge.wait()
    load_back.wait()
    for r, (dx, dy) in enumerate(OFFSETS):
        there = inside(gx, gy, -dx, -dy)
        for h in range(HALO):
            gf[sends[0, 0, h, r]] += back[r * HALO + h] * there
    move_act.wait()


def shaped(shape, dtype=F32):
    return jax.ShapeDtypeStruct(shape, dtype)


def per_device(features, weights, kernel_map, send_lists, counts, cotangent):
    send_lists = jnp.swapaxes(send_lists, 2, 3)
    dma = pltpu.SemaphoreType.DMA
    vmem = pltpu.VMEM
    act, ge, back, summed = pl.pallas_call(
        main_kernel,
        out_shape=(
            shaped((TILES, C, V)),
            shaped((TILES, C, V)),
            shaped((8 * HALO, C, V)),
            shaped((2, NB, 32, 128)),
        ),
        in_specs=[SMEM, SMEM, SMEM, VMEM, ANY, ANY, ANY],
        out_specs=(ANY, ANY, ANY, ANY),
        scratch_shapes=[
            vmem((TILES, C, V), F32),
            vmem((OFFS, C, C), F32),
            vmem((TILES, C, V), F32),
            vmem((WIDE, C, V), BF16),
            vmem((WIDE, C, V), BF16),
            vmem((2 * C, KC), BF16),
            vmem((KC, 4 * C), BF16),
            vmem((8 * HALO, C, V), F32),
            vmem((8 * HALO, C, V), F32),
            vmem((KC, 2 * V), BF16),
            vmem((KC, 2 * V), BF16),
            vmem((KC, 2 * V), BF16),
            vmem((KC, 2 * V), BF16),
            vmem((C, KC), F32),
            vmem((TILES // 2, 2 * C, 2 * V), BF16),
            vmem((ENTRIES, C, V), F32),
            vmem((ENTRIES, C, V), F32),
            vmem((8, RANKS), jnp.int32),
            vmem((8, 128), jnp.int32),
            pltpu.SMEM((8, RANKS), jnp.int32),
            pltpu.SMEM((8, 128), jnp.int32),
            vmem((NB, 32, 128), F32),
            vmem((NB, 32, 128), F32),
            vmem((NB, 32, 128), F32),
            vmem((NB, 32, 128), F32),
            vmem((PLANE, 32, 128), F32),
            vmem((DEEP, 32, 128), F32),
            vmem((NB, 32, 128), F32),
            dma((3,)),
            dma((3,)),
            dma((2,)),
            dma((8,)),
            dma((8,)),
            dma((8,)),
            dma((8,)),
            dma,
            dma,
            dma((NB,)),
            dma((PLANE,)),
            dma((DEEP,)),
            dma((DEEP,)),
            dma((PLANE,)),
            dma((NB,)),
            dma,
            dma,
        ],
        compiler_params=pltpu.CompilerParams(collective_id=0, has_side_effects=True, vmem_limit_bytes=60 << 20),
    )(kernel_map, send_lists, counts, kernel_map, features, weights, cotangent)
    act, gf, gwo = pl.pallas_call(
        finish_kernel,
        out_shape=(shaped((TILES, C, V)), shaped((TILES, C, V)), shaped((OFFS, C, C))),
        in_specs=[SMEM, ANY, ANY, ANY, ANY],
        out_specs=(VMEM, VMEM, VMEM),
        scratch_shapes=[
            vmem((8 * HALO, C, V), F32),
            vmem((2, NB, 32, 128), F32),
            dma((4,)),
        ],
        compiler_params=pltpu.CompilerParams(vmem_limit_bytes=60 << 20),
    )(send_lists, ge, back, summed, act)
    return act[None, None], gf[None, None], gwo


def solution(mesh):
    placed = (
        P("gx", "gy", None, None, None),
        P(),
        P("gx", "gy", None, None),
        P("gx", "gy", None, None),
        P("gx", "gy"),
        P("gx", "gy", None, None, None),
    )
    return jax.shard_map(
        per_device,
        mesh=mesh,
        in_specs=placed,
        out_specs=(P("gx", "gy", None, None, None), P("gx", "gy", None, None, None), P()),
        check_vma=False,
    )
```

```python
import jax
import jax.numpy as jnp
from jax import lax
from jax.experimental import pallas as pl
from jax.experimental.pallas import tpu as pltpu
from jax.sharding import PartitionSpec as P

OFFSETS = ((-1, -1), (-1, 0), (-1, 1), (0, -1), (0, 1), (1, -1), (1, 0), (1, 1))
NX, NY = 32, 8
TILES, HALO, OFFS, C, V = 24, 4, 27, 64, 128
WIDE = TILES + 8 * HALO + 1
KC = 28 * C
NB = KC // 128
PLANE, DEEP = 16, 8
QUAD = 4
HALFWAY = 40
EARLY = (0, 2, 5, 7)
LATE = (3, 4, 1, 6)
ENTRIES = TILES * OFFS
RANKS = 768
MESH = pl.DeviceIdType.MESH
F32, BF16 = jnp.float32, jnp.bfloat16
VMEM = pl.BlockSpec(memory_space=pltpu.VMEM)
ANY = pl.BlockSpec(memory_space=pl.ANY)
SMEM = pl.BlockSpec(memory_space=pltpu.SMEM)


def position():
    return lax.axis_index("gx"), lax.axis_index("gy")


def beside(gx, gy, dx, dy):
    return lax.rem(gx + (dx + NX), NX), lax.rem(gy + (dy + NY), NY)


def inside(gx, gy, dx, dy):
    ok = (gx + dx >= 0) & (gx + dx < NX) & (gy + dy >= 0) & (gy + dy < NY)
    return jnp.where(ok, 1.0, 0.0).astype(F32)


def halves(value):
    high = value.astype(BF16)
    return high, (value - high.astype(F32)).astype(BF16)


def main_kernel(
    kmap,
    sends,
    counts,
    kmap_rows,
    feat_hbm,
    weights_hbm,
    cot_hbm,
    act_hbm,
    ge_hbm,
    back,
    out,
    feat,
    weights,
    cot,
    xh,
    xl,
    wcat,
    wback,
    box,
    inbox,
    catch,
    catl,
    nexth,
    nextl,
    total,
    stacked,
    parts,
    runs,
    order_v,
    upto_v,
    order,
    upto,
    mine,
    theirs,
    given,
    summed,
    xy_in,
    z_in,
    half,
    load_sem,
    store_sem,
    table_sem,
    in_s,
    in_r,
    halo_s,
    halo_r,
    core_s,
    core_r,
    xy_s,
    xy_r,
    fold_s,
    fold_r,
    spread_s,
    spread_r,
    end_s,
    end_r,
):
    gx, gy = position()
    core, z = lax.rem(gx, 2), gx // 4
    xy = (lax.rem(gx // 2, 2) * 2 + gy // 4) * 4 + lax.rem(gy, 4)

    def xy_device(u):
        return (z * 4 + (u // 8) * 2 + core, lax.rem(u // 4, 2) * 4 + lax.rem(u, 4))

    def z_device(d):
        return (lax.rem(z + d, DEEP) * 4 + lax.rem(gx, 4), gy)

    other = (gx + 1 - 2 * core, gy)
    load_feat = pltpu.make_async_copy(feat_hbm.at[0, 0], feat, load_sem.at[0])
    load_weights = pltpu.make_async_copy(weights_hbm, weights, load_sem.at[1])
    load_cot = pltpu.make_async_copy(cot_hbm.at[0, 0], cot, load_sem.at[2])
    load_feat.start()
    load_weights.start()
    load_cot.start()
    barrier = pltpu.get_barrier_semaphore()

    def greet(device):
        pl.semaphore_signal(barrier, inc=1, device_id=device, device_id_type=MESH)

    for d in range(1, DEEP):
        greet(z_device(d))
    for dx, dy in OFFSETS:
        if dx != 0:
            greet(beside(gx, gy, dx, dy))
    for u in range(PLANE):
        pl.when(xy != u)(lambda u=u: greet(xy_device(u)))

    def send(src, dst, send_sem, recv_sem, device):
        return pltpu.make_async_remote_copy(
            src_ref=src, dst_ref=dst, send_sem=send_sem, recv_sem=recv_sem, device_id=device, device_id_type=MESH
        )

    load_feat.wait()
    for r in range(8):
        for h in range(HALO):
            box[r * HALO + h] = feat[sends[0, 0, h, r]]
    pl.semaphore_wait(barrier, 6 + PLANE - 1 + DEEP - 1)
    arriving = []
    for r, (dx, dy) in enumerate(OFFSETS):
        block = pl.ds(r * HALO, HALO)
        copy = send(box.at[block], inbox.at[block], in_s.at[r], in_r.at[r], beside(gx, gy, -dx, -dy))
        copy.start()
        arriving.append(copy)

    load_weights.wait()
    for m in range(NB):
        left = weights[2 * m]
        right = weights[2 * m + 1] if 2 * m + 1 < OFFS else jnp.zeros((C, C), F32)
        pair = jnp.concatenate([left, right], axis=1)
        high, low = halves(pair)
        wcat[0:C, m * 128 : m * 128 + 128] = high
        wcat[C : 2 * C, m * 128 : m * 128 + 128] = low
        turned = pair.T
        high = turned.astype(BF16).astype(F32)
        both = jnp.concatenate([high, turned - high], axis=1).astype(BF16)
        wback[m * 128 : m * 128 + 128, 0:128] = both
        wback[m * 128 : m * 128 + 128, 128:256] = both

    def split_tile(t, carry):
        xh[t], xl[t] = halves(feat[t])
        return carry

    lax.fori_loop(0, TILES, split_tile, 0)
    xh[WIDE - 1] = jnp.zeros((C, V), BF16)
    xl[WIDE - 1] = jnp.zeros((C, V), BF16)
    total[...] = jnp.zeros_like(total)
    for panel in (catch, catl, nexth, nextl):
        panel[OFFS * C : KC, :] = jnp.zeros((C, 2 * V), BF16)

    place = lax.broadcasted_iota(jnp.int32, (TILES, OFFS), 0) * OFFS + lax.broadcasted_iota(jnp.int32, (TILES, OFFS), 1)
    keys = kmap_rows[0, 0] * 1024 + place
    lanes = lax.broadcasted_iota(jnp.int32, (8, 128), 1)

    def rank_row(t, carry):
        ranks, below = carry
        for k in range(OFFS):
            entry = kmap[0, 0, t, k]
            ranks = ranks + jnp.where(keys > entry * 1024 + (t * OFFS + k), 1, 0)
            below = below + jnp.where(lanes >= entry, 1, 0)
        return ranks, below

    ranks, below = lax.fori_loop(
        0, TILES, rank_row, (jnp.zeros((TILES, OFFS), jnp.int32), jnp.zeros((8, 128), jnp.int32))
    )
    upto_v[...] = below
    spots = lax.broadcasted_iota(jnp.int32, (TILES, RANKS), 1)
    found = jnp.zeros((TILES, RANKS), jnp.int32)
    for k in range(OFFS):
        found = found + jnp.where(ranks[:, k : k + 1] == spots, keys[:, k : k + 1], 0)
    order_v[...] = jnp.broadcast_to(jnp.sum(found, axis=0, keepdims=True), (8, RANKS))
    tables = [
        pltpu.make_async_copy(order_v, order, table_sem.at[0]),
        pltpu.make_async_copy(upto_v, upto, table_sem.at[1]),
    ]
    for table in tables:
        table.start()
    load_cot.wait()
    for r, (dx, dy) in enumerate(OFFSETS):
        arriving[r].wait_recv()
        there = inside(gx, gy, dx, dy)
        for h in range(HALO):
            slot = r * HALO + h
            xh[TILES + slot], xl[TILES + slot] = halves(inbox[slot] * there)
    for copy in arriving:
        copy.wait_send()
    for table in tables:
        table.wait()

    contract_last = (((1,), (1,)), ((), ()))

    even, odd = (catch, catl), (nexth, nextl)
    pairs = TILES // 2

    def fill(p, panels):
        for k in range(OFFS):
            for h in range(2):
                slot = kmap[0, 0, p * 2 + h, k]
                panels[0][k * C : k * C + C, h * V : h * V + V] = xh[slot]
                panels[1][k * C : k * C + C, h * V : h * V + V] = xl[slot]

    def product(panels):
        first = jnp.dot(wcat[...], panels[0][...], preferred_element_type=F32)
        second = jnp.dot(wcat[0:C, :], panels[1][...], preferred_element_type=F32)
        return first[0:C] + first[C:] + second

    def activate(p, pre):
        sig = jax.nn.sigmoid(pre)
        slope = sig * (1.0 + pre * (1.0 - sig))
        value = pre * sig
        grads = []
        for h in range(2):
            tile = p * 2 + h
            live = jnp.where(tile < counts[0, 0], 1.0, 0.0).astype(F32)
            feat[tile] = value[:, h * V : h * V + V] * live
            grads.append(cot[tile] * live * slope[:, h * V : h * V + V])
        gh, gl = halves(jnp.concatenate(grads, axis=1))
        stacked[p, 0:C] = gh
        stacked[p, C : 2 * C] = gl

    def weigh(p, panels):
        two = lax.dot_general(stacked[p], panels[0][...], contract_last, preferred_element_type=F32)
        one = lax.dot_general(stacked[p, 0:C], panels[1][...], contract_last, preferred_element_type=F32)
        total[...] += two[0:C] + two[C:] + one

    def advance(p, panels, last):
        fill(p, panels)
        pre = product(panels)
        weigh(p - 1, last)
        activate(p, pre)

    def two_pairs(i, carry):
        advance(2 * i + 1, odd, even)
        advance(2 * i + 2, even, odd)
        return carry

    fill(0, even)
    activate(0, product(even))
    lax.fori_loop(0, pairs // 2 - 1, two_pairs, 0)
    advance(pairs - 1, odd, even)
    weigh(pairs - 1, odd)
    store_act = pltpu.make_async_copy(feat, act_hbm, store_sem.at[0])
    store_act.start()
    core_copy = send(theirs, given, core_s, core_r, other)

    def fold_copy(m, source):
        return send(summed.at[m], xy_in.at[source], xy_s.at[m], xy_r.at[source], xy_device(m))

    def z_copy(d, source):
        return send(z_in.at[source], z_in.at[source], fold_s.at[d], fold_r.at[source], z_device(d))

    def spread_copy(u, m):
        return send(half.at[m], half.at[m], spread_s.at[u], spread_r.at[m], xy_device(u))

    reducer = xy < NB
    own = jnp.minimum(xy, NB - 1)

    def pieces(act):
        for m in range(NB):
            pl.when(xy != m)(lambda m=m: act(m))

    def others(act):
        for u in range(PLANE):
            pl.when(xy != u)(lambda u=u: act(u))

    def tree(values):
        while len(values) > 1:
            values = [values[i] + values[i + 1] for i in range(0, len(values) - 1, 2)] + values[len(values) & ~1 :]
        return values[0]

    for c in range(2):

        @pl.when(core == c)
        def _(c=c):
            for m in range(NB):
                mine[m] = total[c * 32 : c * 32 + 32, m * 128 : m * 128 + 128]
                theirs[m] = total[32 - c * 32 : 64 - c * 32, m * 128 : m * 128 + 128]

    core_copy.start()

    def backward(p, carry):
        gh = jnp.concatenate([stacked[2 * p, 0:C], stacked[2 * p + 1, 0:C]], axis=1)
        gl = jnp.concatenate([stacked[2 * p, C : 2 * C], stacked[2 * p + 1, C : 2 * C]], axis=1)
        four = jnp.concatenate([gh, gh, gl, gl], axis=0)
        for k in range(OFFS):
            part = jnp.dot(wback[k * C : k * C + C, :], four, preferred_element_type=F32)
            for h in range(QUAD):
                parts[(p * QUAD + h) * OFFS + k] = part[:, h * V : h * V + V]
        return carry

    lax.fori_loop(0, 2, backward, 0)
    core_copy.wait_recv()
    summed[...] = mine[...] + given[...]
    pieces(lambda m: fold_copy(m, xy).start())
    xy_in[xy] = summed[own]
    lax.fori_loop(2, TILES // QUAD, backward, 0)

    def scan(step, carry):
        acc, last = carry
        for i in range(8):
            spot = step * 8 + i
            key = order[0, spot]
            entry = lax.shift_right_logical(key, 10)
            same = jnp.where(entry == last, 1.0, 0.0).astype(F32)
            acc = acc * same + parts[lax.bitwise_and(key, 1023)]
            runs[spot] = acc
            last = entry
        return acc, last

    midway = lax.fori_loop(0, HALFWAY, scan, (jnp.zeros((C, V), F32), jnp.int32(WIDE)))

    @pl.when(reducer)
    def _():
        others(lambda u: fold_copy(0, u).wait_recv())
        z_in[z] = tree([xy_in[u] for u in range(PLANE)])
        for d in range(1, DEEP):
            z_copy(d, z).start()

    lax.fori_loop(HALFWAY, ENTRIES // 8, scan, midway)

    def gathered(entry):
        stop = upto[0, entry]
        begin = upto[0, entry - 1] if entry > 0 else jnp.int32(0)
        return runs[jnp.maximum(stop - 1, 0)] * jnp.where(stop > begin, 1.0, 0.0).astype(F32)

    leaving = []

    def leave(r, dx, dy):
        for h in range(HALO):
            box[r * HALO + h] = gathered(TILES + r * HALO + h)
        block = pl.ds(r * HALO, HALO)
        copy = send(box.at[block], back.at[block], halo_s.at[r], halo_r.at[r], beside(gx, gy, dx, dy))
        copy.start()
        leaving.append(copy)

    for r in EARLY:
        leave(r, *OFFSETS[r])

    @pl.when(reducer)
    def _():
        for d in range(1, DEEP):
            z_copy(d, lax.rem(z + d, DEEP)).wait_recv()
        half[own] = tree([z_in[d] for d in range(DEEP)])
        others(lambda u: spread_copy(u, own).start())

    for r in LATE:
        leave(r, *OFFSETS[r])
    for t in range(TILES):
        cot[t] = gathered(t)
    store_ge = pltpu.make_async_copy(cot, ge_hbm, store_sem.at[1])
    store_ge.start()
    pieces(lambda m: spread_copy(0, m).wait_recv())
    end = send(half, out.at[core], end_s, end_r, other)
    end.start()
    store_half = pltpu.make_async_copy(half, out.at[core], store_sem.at[2])
    store_half.start()
    core_copy.wait_send()
    pieces(lambda m: fold_copy(m, xy).wait_send())

    @pl.when(reducer)
    def _():
        for d in range(1, DEEP):
            z_copy(d, z).wait_send()
        others(lambda u: spread_copy(u, own).wait_send())

    store_act.wait()
    store_ge.wait()
    store_half.wait()
    for copy in leaving:
        copy.wait()
    end.wait()


def finish_kernel(sends, ge_hbm, back_hbm, summed_hbm, act_hbm, acts_hbm, gf_hbm, gwo_hbm, acts, gf, gwo, back, summed, sem):
    gx, gy = position()
    load_sums = pltpu.make_async_copy(summed_hbm, summed, sem.at[0])
    load_ge = pltpu.make_async_copy(ge_hbm, gf, sem.at[1])
    load_back = pltpu.make_async_copy(back_hbm, back, sem.at[2])
    load_act = pltpu.make_async_copy(act_hbm, acts, sem.at[3])
    store_act = pltpu.make_async_copy(acts, acts_hbm, sem.at[4])
    store_gwo = pltpu.make_async_copy(gwo, gwo_hbm, sem.at[5])
    store_gf = pltpu.make_async_copy(gf, gf_hbm, sem.at[6])
    for copy in (load_sums, load_act, load_ge, load_back):
        copy.start()
    load_sums.wait()
    for c in range(2):
        for m in range(NB):
            block = summed[c, m]
            gwo[2 * m, c * 32 : c * 32 + 32, :] = block[:, 0:C]
            if 2 * m + 1 < OFFS:
                gwo[2 * m + 1, c * 32 : c * 32 + 32, :] = block[:, C : 2 * C]
    store_gwo.start()
    load_act.wait()
    store_act.start()
    load_ge.wait()
    load_back.wait()
    for r, (dx, dy) in enumerate(OFFSETS):
        there = inside(gx, gy, -dx, -dy)
        for h in range(HALO):
            gf[sends[0, 0, h, r]] += back[r * HALO + h] * there
    store_gf.start()
    store_act.wait()
    store_gwo.wait()
    store_gf.wait()


def shaped(shape, dtype=F32):
    return jax.ShapeDtypeStruct(shape, dtype)


def per_device(features, weights, kernel_map, send_lists, counts, cotangent):
    send_lists = jnp.swapaxes(send_lists, 2, 3)
    dma = pltpu.SemaphoreType.DMA
    vmem = pltpu.VMEM
    act, ge, back, summed = pl.pallas_call(
        main_kernel,
        out_shape=(
            shaped((TILES, C, V)),
            shaped((TILES, C, V)),
            shaped((8 * HALO, C, V)),
            shaped((2, NB, 32, 128)),
        ),
        in_specs=[SMEM, SMEM, SMEM, VMEM, ANY, ANY, ANY],
        out_specs=(ANY, ANY, ANY, ANY),
        scratch_shapes=[
            vmem((TILES, C, V), F32),
            vmem((OFFS, C, C), F32),
            vmem((TILES, C, V), F32),
            vmem((WIDE, C, V), BF16),
            vmem((WIDE, C, V), BF16),
            vmem((2 * C, KC), BF16),
            vmem((KC, 4 * C), BF16),
            vmem((8 * HALO, C, V), F32),
            vmem((8 * HALO, C, V), F32),
            vmem((KC, 2 * V), BF16),
            vmem((KC, 2 * V), BF16),
            vmem((KC, 2 * V), BF16),
            vmem((KC, 2 * V), BF16),
            vmem((C, KC), F32),
            vmem((TILES // 2, 2 * C, 2 * V), BF16),
            vmem((ENTRIES, C, V), F32),
            vmem((ENTRIES, C, V), F32),
            vmem((8, RANKS), jnp.int32),
            vmem((8, 128), jnp.int32),
            pltpu.SMEM((8, RANKS), jnp.int32),
            pltpu.SMEM((8, 128), jnp.int32),
            vmem((NB, 32, 128), F32),
            vmem((NB, 32, 128), F32),
            vmem((NB, 32, 128), F32),
            vmem((NB, 32, 128), F32),
            vmem((PLANE, 32, 128), F32),
            vmem((DEEP, 32, 128), F32),
            vmem((NB, 32, 128), F32),
            dma((3,)),
            dma((3,)),
            dma((2,)),
            dma((8,)),
            dma((8,)),
            dma((8,)),
            dma((8,)),
            dma,
            dma,
            dma((NB,)),
            dma((PLANE,)),
            dma((DEEP,)),
            dma((DEEP,)),
            dma((PLANE,)),
            dma((NB,)),
            dma,
            dma,
        ],
        compiler_params=pltpu.CompilerParams(collective_id=0, has_side_effects=True, vmem_limit_bytes=60 << 20),
    )(kernel_map, send_lists, counts, kernel_map, features, weights, cotangent)
    act, gf, gwo = pl.pallas_call(
        finish_kernel,
        out_shape=(shaped((TILES, C, V)), shaped((TILES, C, V)), shaped((OFFS, C, C))),
        in_specs=[SMEM, ANY, ANY, ANY, ANY],
        out_specs=(ANY, ANY, ANY),
        scratch_shapes=[
            vmem((TILES, C, V), F32),
            vmem((TILES, C, V), F32),
            vmem((OFFS, C, C), F32),
            vmem((8 * HALO, C, V), F32),
            vmem((2, NB, 32, 128), F32),
            dma((7,)),
        ],
        compiler_params=pltpu.CompilerParams(vmem_limit_bytes=60 << 20),
    )(send_lists, ge, back, summed, act)
    return act[None, None], gf[None, None], gwo


def solution(mesh):
    placed = (
        P("gx", "gy", None, None, None),
        P(),
        P("gx", "gy", None, None),
        P("gx", "gy", None, None),
        P("gx", "gy"),
        P("gx", "gy", None, None, None),
    )
    return jax.shard_map(
        per_device,
        mesh=mesh,
        in_specs=placed,
        out_specs=(P("gx", "gy", None, None, None), P("gx", "gy", None, None, None), P()),
        check_vma=False,
    )
```

```python
import jax
import jax.numpy as jnp
from jax import lax
from jax.experimental import pallas as pl
from jax.experimental.pallas import tpu as pltpu
from jax.sharding import PartitionSpec as P

OFFSETS = ((-1, -1), (-1, 0), (-1, 1), (0, -1), (0, 1), (1, -1), (1, 0), (1, 1))
NX, NY = 32, 8
TILES, HALO, OFFS, C, V = 24, 4, 27, 64, 128
WIDE = TILES + 8 * HALO + 1
KC = 28 * C
NB = KC // 128
PLANE, DEEP = 16, 8
QUAD = 4


def hops(step):
    return min(step, 4 - step)


FAR_FIRST = sorted([(a, b) for a in range(4) for b in range(4) if a or b], key=lambda s: -hops(s[0]) - hops(s[1]))
DEPTHS = (4, 3, 5, 2, 6, 1, 7)
HALFWAY = 40
BEFORE = 2
EARLY = (0, 2, 5, 7)
LATE = (3, 4, 1, 6)
ENTRIES = TILES * OFFS
RANKS = 768
MESH = pl.DeviceIdType.MESH
F32, BF16 = jnp.float32, jnp.bfloat16
VMEM = pl.BlockSpec(memory_space=pltpu.VMEM)
ANY = pl.BlockSpec(memory_space=pl.ANY)
SMEM = pl.BlockSpec(memory_space=pltpu.SMEM)


def position():
    return lax.axis_index("gx"), lax.axis_index("gy")


def beside(gx, gy, dx, dy):
    return lax.rem(gx + (dx + NX), NX), lax.rem(gy + (dy + NY), NY)


def inside(gx, gy, dx, dy):
    ok = (gx + dx >= 0) & (gx + dx < NX) & (gy + dy >= 0) & (gy + dy < NY)
    return jnp.where(ok, 1.0, 0.0).astype(F32)


def halves(value):
    high = value.astype(BF16)
    return high, (value - high.astype(F32)).astype(BF16)


def main_kernel(
    kmap,
    sends,
    counts,
    kmap_rows,
    feat_hbm,
    weights_hbm,
    cot_hbm,
    act_hbm,
    ge_hbm,
    back,
    out,
    feat,
    weights,
    cot,
    xh,
    xl,
    wcat,
    wback,
    box,
    inbox,
    catch,
    catl,
    nexth,
    nextl,
    total,
    stacked,
    parts,
    runs,
    order_v,
    upto_v,
    order,
    upto,
    mine,
    theirs,
    given,
    summed,
    xy_in,
    z_in,
    half,
    load_sem,
    store_sem,
    table_sem,
    in_s,
    in_r,
    halo_s,
    halo_r,
    core_s,
    core_r,
    xy_s,
    xy_r,
    fold_s,
    fold_r,
    spread_s,
    spread_r,
    end_s,
    end_r,
):
    gx, gy = position()
    core, z = lax.rem(gx, 2), gx // 4
    xy = (lax.rem(gx // 2, 2) * 2 + gy // 4) * 4 + lax.rem(gy, 4)

    def xy_device(u):
        return (z * 4 + (u // 8) * 2 + core, lax.rem(u // 4, 2) * 4 + lax.rem(u, 4))

    def z_device(d):
        return (lax.rem(z + d, DEEP) * 4 + lax.rem(gx, 4), gy)

    other = (gx + 1 - 2 * core, gy)
    load_feat = pltpu.make_async_copy(feat_hbm.at[0, 0], feat, load_sem.at[0])
    load_weights = pltpu.make_async_copy(weights_hbm, weights, load_sem.at[1])
    load_cot = pltpu.make_async_copy(cot_hbm.at[0, 0], cot, load_sem.at[2])
    load_feat.start()
    load_weights.start()
    load_cot.start()
    barrier = pltpu.get_barrier_semaphore()

    def greet(device):
        pl.semaphore_signal(barrier, inc=1, device_id=device, device_id_type=MESH)

    for d in range(1, DEEP):
        greet(z_device(d))
    for dx, dy in OFFSETS:
        if dx != 0:
            greet(beside(gx, gy, dx, dy))
    for u in range(PLANE):
        pl.when(xy != u)(lambda u=u: greet(xy_device(u)))

    def send(src, dst, send_sem, recv_sem, device):
        return pltpu.make_async_remote_copy(
            src_ref=src, dst_ref=dst, send_sem=send_sem, recv_sem=recv_sem, device_id=device, device_id_type=MESH
        )

    load_feat.wait()
    for r in range(8):
        for h in range(HALO):
            box[r * HALO + h] = feat[sends[0, 0, h, r]]
    pl.semaphore_wait(barrier, 6 + PLANE - 1 + DEEP - 1)
    arriving = []
    for r, (dx, dy) in enumerate(OFFSETS):
        block = pl.ds(r * HALO, HALO)
        copy = send(box.at[block], inbox.at[block], in_s.at[r], in_r.at[r], beside(gx, gy, -dx, -dy))
        copy.start()
        arriving.append(copy)

    load_weights.wait()
    for m in range(NB):
        left = weights[2 * m]
        right = weights[2 * m + 1] if 2 * m + 1 < OFFS else jnp.zeros((C, C), F32)
        pair = jnp.concatenate([left, right], axis=1)
        high, low = halves(pair)
        wcat[0:C, m * 128 : m * 128 + 128] = high
        wcat[C : 2 * C, m * 128 : m * 128 + 128] = low
        turned = pair.T
        high = turned.astype(BF16).astype(F32)
        both = jnp.concatenate([high, turned - high], axis=1).astype(BF16)
        wback[m * 128 : m * 128 + 128, 0:128] = both
        wback[m * 128 : m * 128 + 128, 128:256] = both

    def split_tile(t, carry):
        xh[t], xl[t] = halves(feat[t])
        return carry

    lax.fori_loop(0, TILES, split_tile, 0)
    xh[WIDE - 1] = jnp.zeros((C, V), BF16)
    xl[WIDE - 1] = jnp.zeros((C, V), BF16)
    total[...] = jnp.zeros_like(total)
    for panel in (catch, catl, nexth, nextl):
        panel[OFFS * C : KC, :] = jnp.zeros((C, 2 * V), BF16)

    place = lax.broadcasted_iota(jnp.int32, (TILES, OFFS), 0) * OFFS + lax.broadcasted_iota(jnp.int32, (TILES, OFFS), 1)
    keys = kmap_rows[0, 0] * 1024 + place
    lanes = lax.broadcasted_iota(jnp.int32, (8, 128), 1)

    def rank_row(t, carry):
        ranks, below = carry
        for k in range(OFFS):
            entry = kmap[0, 0, t, k]
            ranks = ranks + jnp.where(keys > entry * 1024 + (t * OFFS + k), 1, 0)
            below = below + jnp.where(lanes >= entry, 1, 0)
        return ranks, below

    ranks, below = lax.fori_loop(
        0, TILES, rank_row, (jnp.zeros((TILES, OFFS), jnp.int32), jnp.zeros((8, 128), jnp.int32))
    )
    upto_v[...] = below
    spots = lax.broadcasted_iota(jnp.int32, (TILES, RANKS), 1)
    found = jnp.zeros((TILES, RANKS), jnp.int32)
    for k in range(OFFS):
        found = found + jnp.where(ranks[:, k : k + 1] == spots, keys[:, k : k + 1], 0)
    order_v[...] = jnp.broadcast_to(jnp.sum(found, axis=0, keepdims=True), (8, RANKS))
    tables = [
        pltpu.make_async_copy(order_v, order, table_sem.at[0]),
        pltpu.make_async_copy(upto_v, upto, table_sem.at[1]),
    ]
    for table in tables:
        table.start()
    load_cot.wait()
    for r, (dx, dy) in enumerate(OFFSETS):
        arriving[r].wait_recv()
        there = inside(gx, gy, dx, dy)
        for h in range(HALO):
            slot = r * HALO + h
            xh[TILES + slot], xl[TILES + slot] = halves(inbox[slot] * there)
    for copy in arriving:
        copy.wait_send()
    for table in tables:
        table.wait()

    contract_last = (((1,), (1,)), ((), ()))

    even, odd = (catch, catl), (nexth, nextl)
    pairs = TILES // 2

    def fill(p, panels):
        for k in range(OFFS):
            for h in range(2):
                slot = kmap[0, 0, p * 2 + h, k]
                panels[0][k * C : k * C + C, h * V : h * V + V] = xh[slot]
                panels[1][k * C : k * C + C, h * V : h * V + V] = xl[slot]

    def product(panels):
        first = jnp.dot(wcat[...], panels[0][...], preferred_element_type=F32)
        second = jnp.dot(wcat[0:C, :], panels[1][...], preferred_element_type=F32)
        return first[0:C] + first[C:] + second

    def activate(p, pre):
        sig = jax.nn.sigmoid(pre)
        slope = sig * (1.0 + pre * (1.0 - sig))
        value = pre * sig
        grads = []
        for h in range(2):
            tile = p * 2 + h
            live = jnp.where(tile < counts[0, 0], 1.0, 0.0).astype(F32)
            feat[tile] = value[:, h * V : h * V + V] * live
            grads.append(cot[tile] * live * slope[:, h * V : h * V + V])
        gh, gl = halves(jnp.concatenate(grads, axis=1))
        stacked[p, 0:C] = gh
        stacked[p, C : 2 * C] = gl

    def weigh(p, panels):
        two = lax.dot_general(stacked[p], panels[0][...], contract_last, preferred_element_type=F32)
        one = lax.dot_general(stacked[p, 0:C], panels[1][...], contract_last, preferred_element_type=F32)
        total[...] += two[0:C] + two[C:] + one

    def advance(p, panels, last):
        fill(p, panels)
        pre = product(panels)
        weigh(p - 1, last)
        activate(p, pre)

    def two_pairs(i, carry):
        advance(2 * i + 1, odd, even)
        advance(2 * i + 2, even, odd)
        return carry

    fill(0, even)
    activate(0, product(even))
    lax.fori_loop(0, pairs // 2 - 1, two_pairs, 0)
    advance(pairs - 1, odd, even)
    weigh(pairs - 1, odd)
    store_act = pltpu.make_async_copy(feat, act_hbm, store_sem.at[0])
    store_act.start()
    core_copy = send(theirs, given, core_s, core_r, other)

    def fold_copy(m, source):
        return send(summed.at[m], xy_in.at[source], xy_s.at[m], xy_r.at[source], xy_device(m))

    def z_copy(d, source):
        return send(z_in.at[source], z_in.at[source], fold_s.at[d], fold_r.at[source], z_device(d))

    def spread_copy(u, m):
        return send(half.at[m], half.at[m], spread_s.at[u], spread_r.at[m], xy_device(u))

    reducer = xy < NB
    own = jnp.minimum(xy, NB - 1)

    def pieces(act):
        for m in members():
            pl.when(m < NB)(lambda m=m: act(m))

    row, column = xy // 4, lax.rem(xy, 4)

    def members():
        return [lax.rem(row + a, 4) * 4 + lax.rem(column + b, 4) for a, b in FAR_FIRST]

    def others(act):
        for u in members():
            act(u)

    def tree(values):
        while len(values) > 1:
            values = [values[i] + values[i + 1] for i in range(0, len(values) - 1, 2)] + values[len(values) & ~1 :]
        return values[0]

    for c in range(2):

        @pl.when(core == c)
        def _(c=c):
            for m in range(NB):
                mine[m] = total[c * 32 : c * 32 + 32, m * 128 : m * 128 + 128]
                theirs[m] = total[32 - c * 32 : 64 - c * 32, m * 128 : m * 128 + 128]

    core_copy.start()

    def backward(p, carry):
        gh = jnp.concatenate([stacked[2 * p, 0:C], stacked[2 * p + 1, 0:C]], axis=1)
        gl = jnp.concatenate([stacked[2 * p, C : 2 * C], stacked[2 * p + 1, C : 2 * C]], axis=1)
        four = jnp.concatenate([gh, gh, gl, gl], axis=0)
        for k in range(OFFS):
            part = jnp.dot(wback[k * C : k * C + C, :], four, preferred_element_type=F32)
            for h in range(QUAD):
                parts[(p * QUAD + h) * OFFS + k] = part[:, h * V : h * V + V]
        return carry

    lax.fori_loop(0, BEFORE, backward, 0)
    core_copy.wait_recv()
    summed[...] = mine[...] + given[...]
    pieces(lambda m: fold_copy(m, xy).start())
    xy_in[xy] = summed[own]
    lax.fori_loop(BEFORE, TILES // QUAD, backward, 0)

    def scan(step, carry):
        acc, last = carry
        for i in range(8):
            spot = step * 8 + i
            key = order[0, spot]
            entry = lax.shift_right_logical(key, 10)
            same = jnp.where(entry == last, 1.0, 0.0).astype(F32)
            acc = acc * same + parts[lax.bitwise_and(key, 1023)]
            runs[spot] = acc
            last = entry
        return acc, last

    midway = lax.fori_loop(0, HALFWAY, scan, (jnp.zeros((C, V), F32), jnp.int32(WIDE)))

    @pl.when(reducer)
    def _():
        others(lambda u: fold_copy(0, u).wait_recv())
        z_in[z] = tree([xy_in[u] for u in range(PLANE)])
        for d in DEPTHS:
            z_copy(d, z).start()

    lax.fori_loop(HALFWAY, ENTRIES // 8, scan, midway)

    def gathered(entry):
        stop = upto[0, entry]
        begin = upto[0, entry - 1] if entry > 0 else jnp.int32(0)
        return runs[jnp.maximum(stop - 1, 0)] * jnp.where(stop > begin, 1.0, 0.0).astype(F32)

    leaving = []

    def leave(r, dx, dy):
        for h in range(HALO):
            box[r * HALO + h] = gathered(TILES + r * HALO + h)
        block = pl.ds(r * HALO, HALO)
        copy = send(box.at[block], back.at[block], halo_s.at[r], halo_r.at[r], beside(gx, gy, dx, dy))
        copy.start()
        leaving.append(copy)

    for r in EARLY:
        leave(r, *OFFSETS[r])

    @pl.when(reducer)
    def _():
        for d in range(1, DEEP):
            z_copy(d, lax.rem(z + d, DEEP)).wait_recv()
        half[own] = tree([z_in[d] for d in range(DEEP)])
        others(lambda u: spread_copy(u, own).start())

    for r in LATE:
        leave(r, *OFFSETS[r])
    for t in range(TILES):
        cot[t] = gathered(t)
    store_ge = pltpu.make_async_copy(cot, ge_hbm, store_sem.at[1])
    store_ge.start()
    pieces(lambda m: spread_copy(0, m).wait_recv())
    end = send(half, out.at[core], end_s, end_r, other)
    end.start()
    store_half = pltpu.make_async_copy(half, out.at[core], store_sem.at[2])
    store_half.start()
    core_copy.wait_send()
    pieces(lambda m: fold_copy(m, xy).wait_send())

    @pl.when(reducer)
    def _():
        for d in range(1, DEEP):
            z_copy(d, z).wait_send()
        others(lambda u: spread_copy(u, own).wait_send())

    store_act.wait()
    store_ge.wait()
    store_half.wait()
    for copy in leaving:
        copy.wait()
    end.wait()


def finish_kernel(sends, ge_hbm, back_hbm, summed_hbm, act_hbm, acts_hbm, gf_hbm, gwo_hbm, acts, gf, gwo, back, summed, sem):
    gx, gy = position()
    load_sums = pltpu.make_async_copy(summed_hbm, summed, sem.at[0])
    load_ge = pltpu.make_async_copy(ge_hbm, gf, sem.at[1])
    load_back = pltpu.make_async_copy(back_hbm, back, sem.at[2])
    load_act = pltpu.make_async_copy(act_hbm, acts, sem.at[3])
    store_act = pltpu.make_async_copy(acts, acts_hbm, sem.at[4])
    store_gwo = pltpu.make_async_copy(gwo, gwo_hbm, sem.at[5])
    store_gf = pltpu.make_async_copy(gf, gf_hbm, sem.at[6])
    for copy in (load_sums, load_act, load_ge, load_back):
        copy.start()
    load_sums.wait()
    for c in range(2):
        for m in range(NB):
            block = summed[c, m]
            gwo[2 * m, c * 32 : c * 32 + 32, :] = block[:, 0:C]
            if 2 * m + 1 < OFFS:
                gwo[2 * m + 1, c * 32 : c * 32 + 32, :] = block[:, C : 2 * C]
    store_gwo.start()
    load_act.wait()
    store_act.start()
    load_ge.wait()
    load_back.wait()
    for r, (dx, dy) in enumerate(OFFSETS):
        there = inside(gx, gy, -dx, -dy)
        for h in range(HALO):
            gf[sends[0, 0, h, r]] += back[r * HALO + h] * there
    store_gf.start()
    store_act.wait()
    store_gwo.wait()
    store_gf.wait()


def shaped(shape, dtype=F32):
    return jax.ShapeDtypeStruct(shape, dtype)


def per_device(features, weights, kernel_map, send_lists, counts, cotangent):
    send_lists = jnp.swapaxes(send_lists, 2, 3)
    dma = pltpu.SemaphoreType.DMA
    vmem = pltpu.VMEM
    act, ge, back, summed = pl.pallas_call(
        main_kernel,
        out_shape=(
            shaped((TILES, C, V)),
            shaped((TILES, C, V)),
            shaped((8 * HALO, C, V)),
            shaped((2, NB, 32, 128)),
        ),
        in_specs=[SMEM, SMEM, SMEM, VMEM, ANY, ANY, ANY],
        out_specs=(ANY, ANY, ANY, ANY),
        scratch_shapes=[
            vmem((TILES, C, V), F32),
            vmem((OFFS, C, C), F32),
            vmem((TILES, C, V), F32),
            vmem((WIDE, C, V), BF16),
            vmem((WIDE, C, V), BF16),
            vmem((2 * C, KC), BF16),
            vmem((KC, 4 * C), BF16),
            vmem((8 * HALO, C, V), F32),
            vmem((8 * HALO, C, V), F32),
            vmem((KC, 2 * V), BF16),
            vmem((KC, 2 * V), BF16),
            vmem((KC, 2 * V), BF16),
            vmem((KC, 2 * V), BF16),
            vmem((C, KC), F32),
            vmem((TILES // 2, 2 * C, 2 * V), BF16),
            vmem((ENTRIES, C, V), F32),
            vmem((ENTRIES, C, V), F32),
            vmem((8, RANKS), jnp.int32),
            vmem((8, 128), jnp.int32),
            pltpu.SMEM((8, RANKS), jnp.int32),
            pltpu.SMEM((8, 128), jnp.int32),
            vmem((NB, 32, 128), F32),
            vmem((NB, 32, 128), F32),
            vmem((NB, 32, 128), F32),
            vmem((NB, 32, 128), F32),
            vmem((PLANE, 32, 128), F32),
            vmem((DEEP, 32, 128), F32),
            vmem((NB, 32, 128), F32),
            dma((3,)),
            dma((3,)),
            dma((2,)),
            dma((8,)),
            dma((8,)),
            dma((8,)),
            dma((8,)),
            dma,
            dma,
            dma((NB,)),
            dma((PLANE,)),
            dma((DEEP,)),
            dma((DEEP,)),
            dma((PLANE,)),
            dma((NB,)),
            dma,
            dma,
        ],
        compiler_params=pltpu.CompilerParams(collective_id=0, has_side_effects=True, vmem_limit_bytes=60 << 20),
    )(kernel_map, send_lists, counts, kernel_map, features, weights, cotangent)
    act, gf, gwo = pl.pallas_call(
        finish_kernel,
        out_shape=(shaped((TILES, C, V)), shaped((TILES, C, V)), shaped((OFFS, C, C))),
        in_specs=[SMEM, ANY, ANY, ANY, ANY],
        out_specs=(ANY, ANY, ANY),
        scratch_shapes=[
            vmem((TILES, C, V), F32),
            vmem((TILES, C, V), F32),
            vmem((OFFS, C, C), F32),
            vmem((8 * HALO, C, V), F32),
            vmem((2, NB, 32, 128), F32),
            dma((7,)),
        ],
        compiler_params=pltpu.CompilerParams(vmem_limit_bytes=60 << 20),
    )(send_lists, ge, back, summed, act)
    return act[None, None], gf[None, None], gwo


def solution(mesh):
    placed = (
        P("gx", "gy", None, None, None),
        P(),
        P("gx", "gy", None, None),
        P("gx", "gy", None, None),
        P("gx", "gy"),
        P("gx", "gy", None, None, None),
    )
    return jax.shard_map(
        per_device,
        mesh=mesh,
        in_specs=placed,
        out_specs=(P("gx", "gy", None, None, None), P("gx", "gy", None, None, None), P()),
        check_vma=False,
    )
```

```python
import jax
import jax.numpy as jnp
from jax import lax
from jax.experimental import pallas as pl
from jax.experimental.pallas import tpu as pltpu
from jax.sharding import PartitionSpec as P

OFFSETS = ((-1, -1), (-1, 0), (-1, 1), (0, -1), (0, 1), (1, -1), (1, 0), (1, 1))
NX, NY = 32, 8
TILES, HALO, OFFS, C, V = 24, 4, 27, 64, 128
WIDE = TILES + 8 * HALO + 1
KC = 28 * C
NB = KC // 128
PLANE, DEEP = 16, 8
QUAD = 4
HALFWAY = 40
EARLY = (0, 2, 5, 7)
LATE = (3, 4, 1, 6)
ENTRIES = TILES * OFFS
RANKS = 768
MESH = pl.DeviceIdType.MESH
F32, BF16 = jnp.float32, jnp.bfloat16
VMEM = pl.BlockSpec(memory_space=pltpu.VMEM)
ANY = pl.BlockSpec(memory_space=pl.ANY)
SMEM = pl.BlockSpec(memory_space=pltpu.SMEM)


def position():
    return lax.axis_index("gx"), lax.axis_index("gy")


def beside(gx, gy, dx, dy):
    return lax.rem(gx + (dx + NX), NX), lax.rem(gy + (dy + NY), NY)


def inside(gx, gy, dx, dy):
    ok = (gx + dx >= 0) & (gx + dx < NX) & (gy + dy >= 0) & (gy + dy < NY)
    return jnp.where(ok, 1.0, 0.0).astype(F32)


def halves(value):
    high = value.astype(BF16)
    return high, (value - high.astype(F32)).astype(BF16)


def main_kernel(
    kmap,
    sends,
    counts,
    kmap_rows,
    feat_hbm,
    weights_hbm,
    cot_hbm,
    act_hbm,
    ge_hbm,
    back,
    out,
    feat,
    weights,
    cot,
    xh,
    xl,
    wcat,
    wback,
    box,
    inbox,
    catch,
    catl,
    nexth,
    nextl,
    total,
    stacked,
    parts,
    runs,
    order_v,
    upto_v,
    order,
    upto,
    mine,
    theirs,
    given,
    summed,
    xy_in,
    z_in,
    half,
    load_sem,
    store_sem,
    table_sem,
    in_s,
    in_r,
    halo_s,
    halo_r,
    core_s,
    core_r,
    xy_s,
    xy_r,
    fold_s,
    fold_r,
    spread_s,
    spread_r,
    end_s,
    end_r,
):
    gx, gy = position()
    core, z = lax.rem(gx, 2), gx // 4
    xy = (lax.rem(gx // 2, 2) * 2 + gy // 4) * 4 + lax.rem(gy, 4)

    def xy_device(u):
        return (z * 4 + (u // 8) * 2 + core, lax.rem(u // 4, 2) * 4 + lax.rem(u, 4))

    def z_device(d):
        return (lax.rem(z + d, DEEP) * 4 + lax.rem(gx, 4), gy)

    other = (gx + 1 - 2 * core, gy)
    load_feat = pltpu.make_async_copy(feat_hbm.at[0, 0], feat, load_sem.at[0])
    load_weights = pltpu.make_async_copy(weights_hbm, weights, load_sem.at[1])
    load_cot = pltpu.make_async_copy(cot_hbm.at[0, 0], cot, load_sem.at[2])
    load_feat.start()
    load_weights.start()
    load_cot.start()
    barrier = pltpu.get_barrier_semaphore()

    def greet(device):
        pl.semaphore_signal(barrier, inc=1, device_id=device, device_id_type=MESH)

    for d in range(1, DEEP):
        greet(z_device(d))
    for dx, dy in OFFSETS:
        if dx != 0:
            greet(beside(gx, gy, dx, dy))
    for u in range(PLANE):
        pl.when(xy != u)(lambda u=u: greet(xy_device(u)))

    def send(src, dst, send_sem, recv_sem, device):
        return pltpu.make_async_remote_copy(
            src_ref=src, dst_ref=dst, send_sem=send_sem, recv_sem=recv_sem, device_id=device, device_id_type=MESH
        )

    load_feat.wait()
    for r in range(8):
        for h in range(HALO):
            box[r * HALO + h] = feat[sends[0, 0, h, r]]
    pl.semaphore_wait(barrier, 6 + PLANE - 1 + DEEP - 1)
    arriving = []
    for r, (dx, dy) in enumerate(OFFSETS):
        block = pl.ds(r * HALO, HALO)
        copy = send(box.at[block], inbox.at[block], in_s.at[r], in_r.at[r], beside(gx, gy, -dx, -dy))
        copy.start()
        arriving.append(copy)

    load_weights.wait()
    for m in range(NB):
        left = weights[2 * m]
        right = weights[2 * m + 1] if 2 * m + 1 < OFFS else jnp.zeros((C, C), F32)
        pair = jnp.concatenate([left, right], axis=1)
        high, low = halves(pair)
        wcat[0:C, m * 128 : m * 128 + 128] = high
        wcat[C : 2 * C, m * 128 : m * 128 + 128] = low
        turned = pair.T
        high = turned.astype(BF16).astype(F32)
        both = jnp.concatenate([high, turned - high], axis=1).astype(BF16)
        wback[m * 128 : m * 128 + 128, 0:128] = both
        wback[m * 128 : m * 128 + 128, 128:256] = both

    def split_tile(t, carry):
        xh[t], xl[t] = halves(feat[t])
        return carry

    lax.fori_loop(0, TILES, split_tile, 0)
    xh[WIDE - 1] = jnp.zeros((C, V), BF16)
    xl[WIDE - 1] = jnp.zeros((C, V), BF16)
    total[...] = jnp.zeros_like(total)
    for panel in (catch, catl, nexth, nextl):
        panel[OFFS * C : KC, :] = jnp.zeros((C, 2 * V), BF16)

    place = lax.broadcasted_iota(jnp.int32, (TILES, OFFS), 0) * OFFS + lax.broadcasted_iota(jnp.int32, (TILES, OFFS), 1)
    keys = kmap_rows[0, 0] * 1024 + place
    lanes = lax.broadcasted_iota(jnp.int32, (8, 128), 1)

    def rank_row(t, carry):
        ranks, below = carry
        for k in range(OFFS):
            entry = kmap[0, 0, t, k]
            ranks = ranks + jnp.where(keys > entry * 1024 + (t * OFFS + k), 1, 0)
            below = below + jnp.where(lanes >= entry, 1, 0)
        return ranks, below

    ranks, below = lax.fori_loop(
        0, TILES, rank_row, (jnp.zeros((TILES, OFFS), jnp.int32), jnp.zeros((8, 128), jnp.int32))
    )
    upto_v[...] = below
    spots = lax.broadcasted_iota(jnp.int32, (TILES, RANKS), 1)
    found = jnp.zeros((TILES, RANKS), jnp.int32)
    for k in range(OFFS):
        found = found + jnp.where(ranks[:, k : k + 1] == spots, keys[:, k : k + 1], 0)
    order_v[...] = jnp.broadcast_to(jnp.sum(found, axis=0, keepdims=True), (8, RANKS))
    tables = [
        pltpu.make_async_copy(order_v, order, table_sem.at[0]),
        pltpu.make_async_copy(upto_v, upto, table_sem.at[1]),
    ]
    for table in tables:
        table.start()
    load_cot.wait()
    for r, (dx, dy) in enumerate(OFFSETS):
        arriving[r].wait_recv()
        there = inside(gx, gy, dx, dy)
        for h in range(HALO):
            slot = r * HALO + h
            xh[TILES + slot], xl[TILES + slot] = halves(inbox[slot] * there)
    for copy in arriving:
        copy.wait_send()
    for table in tables:
        table.wait()

    contract_last = (((1,), (1,)), ((), ()))

    even, odd = (catch, catl), (nexth, nextl)
    pairs = TILES // 2

    def fill(p, panels):
        for k in range(OFFS):
            for h in range(2):
                slot = kmap[0, 0, p * 2 + h, k]
                panels[0][k * C : k * C + C, h * V : h * V + V] = xh[slot]
                panels[1][k * C : k * C + C, h * V : h * V + V] = xl[slot]

    def product(panels):
        first = jnp.dot(wcat[...], panels[0][...], preferred_element_type=F32)
        second = jnp.dot(wcat[0:C, :], panels[1][...], preferred_element_type=F32)
        return first[0:C] + first[C:] + second

    def activate(p, pre):
        sig = jax.nn.sigmoid(pre)
        slope = sig * (1.0 + pre * (1.0 - sig))
        value = pre * sig
        grads = []
        for h in range(2):
            tile = p * 2 + h
            live = jnp.where(tile < counts[0, 0], 1.0, 0.0).astype(F32)
            feat[tile] = value[:, h * V : h * V + V] * live
            grads.append(cot[tile] * live * slope[:, h * V : h * V + V])
        gh, gl = halves(jnp.concatenate(grads, axis=1))
        stacked[p, 0:C] = gh
        stacked[p, C : 2 * C] = gl

    def weigh(p, panels):
        two = lax.dot_general(stacked[p], panels[0][...], contract_last, preferred_element_type=F32)
        one = lax.dot_general(stacked[p, 0:C], panels[1][...], contract_last, preferred_element_type=F32)
        total[...] += two[0:C] + two[C:] + one

    def advance(p, panels, last):
        fill(p, panels)
        pre = product(panels)
        weigh(p - 1, last)
        activate(p, pre)

    def two_pairs(i, carry):
        advance(2 * i + 1, odd, even)
        advance(2 * i + 2, even, odd)
        return carry

    fill(0, even)
    activate(0, product(even))
    lax.fori_loop(0, pairs // 2 - 1, two_pairs, 0)
    advance(pairs - 1, odd, even)
    weigh(pairs - 1, odd)
    store_act = pltpu.make_async_copy(feat, act_hbm, store_sem.at[0])
    store_act.start()
    core_copy = send(theirs, given, core_s, core_r, other)

    def fold_copy(m, source):
        return send(summed.at[m], xy_in.at[source], xy_s.at[m], xy_r.at[source], xy_device(m))

    def z_copy(d, source):
        return send(z_in.at[source], z_in.at[source], fold_s.at[d], fold_r.at[source], z_device(d))

    def spread_copy(u, m):
        return send(half.at[m], half.at[m], spread_s.at[u], spread_r.at[m], xy_device(u))

    reducer = xy < NB
    own = jnp.minimum(xy, NB - 1)

    def pieces(act):
        for m in range(NB):
            pl.when(xy != m)(lambda m=m: act(m))

    def others(act):
        for u in range(PLANE):
            pl.when(xy != u)(lambda u=u: act(u))

    def tree(values):
        while len(values) > 1:
            values = [values[i] + values[i + 1] for i in range(0, len(values) - 1, 2)] + values[len(values) & ~1 :]
        return values[0]

    for c in range(2):

        @pl.when(core == c)
        def _(c=c):
            for m in range(NB):
                mine[m] = total[c * 32 : c * 32 + 32, m * 128 : m * 128 + 128]
                theirs[m] = total[32 - c * 32 : 64 - c * 32, m * 128 : m * 128 + 128]

    core_copy.start()

    def backward(p, carry):
        gh = jnp.concatenate([stacked[2 * p, 0:C], stacked[2 * p + 1, 0:C]], axis=1)
        gl = jnp.concatenate([stacked[2 * p, C : 2 * C], stacked[2 * p + 1, C : 2 * C]], axis=1)
        four = jnp.concatenate([gh, gh, gl, gl], axis=0)
        for k in range(OFFS):
            part = jnp.dot(wback[k * C : k * C + C, :], four, preferred_element_type=F32)
            for h in range(QUAD):
                parts[(p * QUAD + h) * OFFS + k] = part[:, h * V : h * V + V]
        return carry

    lax.fori_loop(0, 2, backward, 0)
    core_copy.wait_recv()
    summed[...] = mine[...] + given[...]
    pieces(lambda m: fold_copy(m, xy).start())
    xy_in[xy] = summed[own]
    lax.fori_loop(2, TILES // QUAD, backward, 0)

    def scan(step, carry):
        acc, last = carry
        for i in range(8):
            spot = step * 8 + i
            key = order[0, spot]
            entry = lax.shift_right_logical(key, 10)
            same = jnp.where(entry == last, 1.0, 0.0).astype(F32)
            acc = acc * same + parts[lax.bitwise_and(key, 1023)]
            runs[spot] = acc
            last = entry
        return acc, last

    midway = lax.fori_loop(0, HALFWAY, scan, (jnp.zeros((C, V), F32), jnp.int32(WIDE)))

    @pl.when(reducer)
    def _():
        others(lambda u: fold_copy(0, u).wait_recv())
        z_in[z] = tree([xy_in[u] for u in range(PLANE)])
        for d in range(1, DEEP):
            z_copy(d, z).start()

    lax.fori_loop(HALFWAY, ENTRIES // 8, scan, midway)

    def gathered(entry):
        stop = upto[0, entry]
        begin = upto[0, entry - 1] if entry > 0 else jnp.int32(0)
        return runs[jnp.maximum(stop - 1, 0)] * jnp.where(stop > begin, 1.0, 0.0).astype(F32)

    leaving = []

    def leave(r, dx, dy):
        for h in range(HALO):
            box[r * HALO + h] = gathered(TILES + r * HALO + h)
        block = pl.ds(r * HALO, HALO)
        copy = send(box.at[block], back.at[block], halo_s.at[r], halo_r.at[r], beside(gx, gy, dx, dy))
        copy.start()
        leaving.append(copy)

    for r in EARLY:
        leave(r, *OFFSETS[r])

    @pl.when(reducer)
    def _():
        for d in range(1, DEEP):
            z_copy(d, lax.rem(z + d, DEEP)).wait_recv()
        half[own] = tree([z_in[d] for d in range(DEEP)])
        others(lambda u: spread_copy(u, own).start())

    for r in LATE:
        leave(r, *OFFSETS[r])
    for t in range(TILES):
        cot[t] = gathered(t)
    store_ge = pltpu.make_async_copy(cot, ge_hbm, store_sem.at[1])
    store_ge.start()
    pieces(lambda m: spread_copy(0, m).wait_recv())
    end = send(half, out.at[core], end_s, end_r, other)
    end.start()
    store_half = pltpu.make_async_copy(half, out.at[core], store_sem.at[2])
    store_half.start()
    core_copy.wait_send()
    pieces(lambda m: fold_copy(m, xy).wait_send())

    @pl.when(reducer)
    def _():
        for d in range(1, DEEP):
            z_copy(d, z).wait_send()
        others(lambda u: spread_copy(u, own).wait_send())

    store_act.wait()
    store_ge.wait()
    store_half.wait()
    for copy in leaving:
        copy.wait()
    end.wait()


def finish_kernel(sends, ge_hbm, back_hbm, summed_hbm, act_hbm, acts_hbm, gf_hbm, gwo_hbm, acts, gf, gwo, back, summed, sem):
    gx, gy = position()
    load_sums = pltpu.make_async_copy(summed_hbm, summed, sem.at[0])
    load_ge = pltpu.make_async_copy(ge_hbm, gf, sem.at[1])
    load_back = pltpu.make_async_copy(back_hbm, back, sem.at[2])
    load_act = pltpu.make_async_copy(act_hbm, acts, sem.at[3])
    store_act = pltpu.make_async_copy(acts, acts_hbm, sem.at[4])
    store_gwo = pltpu.make_async_copy(gwo, gwo_hbm, sem.at[5])
    store_gf = pltpu.make_async_copy(gf, gf_hbm, sem.at[6])
    for copy in (load_ge, load_back, load_sums, load_act):
        copy.start()
    load_ge.wait()
    load_back.wait()
    for r, (dx, dy) in enumerate(OFFSETS):
        there = inside(gx, gy, -dx, -dy)
        for h in range(HALO):
            gf[sends[0, 0, h, r]] += back[r * HALO + h] * there
    store_gf.start()
    load_act.wait()
    store_act.start()
    load_sums.wait()
    for c in range(2):
        for m in range(NB):
            block = summed[c, m]
            gwo[2 * m, c * 32 : c * 32 + 32, :] = block[:, 0:C]
            if 2 * m + 1 < OFFS:
                gwo[2 * m + 1, c * 32 : c * 32 + 32, :] = block[:, C : 2 * C]
    store_gwo.start()
    store_act.wait()
    store_gwo.wait()
    store_gf.wait()


def shaped(shape, dtype=F32):
    return jax.ShapeDtypeStruct(shape, dtype)


def per_device(features, weights, kernel_map, send_lists, counts, cotangent):
    send_lists = jnp.swapaxes(send_lists, 2, 3)
    dma = pltpu.SemaphoreType.DMA
    vmem = pltpu.VMEM
    act, ge, back, summed = pl.pallas_call(
        main_kernel,
        out_shape=(
            shaped((TILES, C, V)),
            shaped((TILES, C, V)),
            shaped((8 * HALO, C, V)),
            shaped((2, NB, 32, 128)),
        ),
        in_specs=[SMEM, SMEM, SMEM, VMEM, ANY, ANY, ANY],
        out_specs=(ANY, ANY, ANY, ANY),
        scratch_shapes=[
            vmem((TILES, C, V), F32),
            vmem((OFFS, C, C), F32),
            vmem((TILES, C, V), F32),
            vmem((WIDE, C, V), BF16),
            vmem((WIDE, C, V), BF16),
            vmem((2 * C, KC), BF16),
            vmem((KC, 4 * C), BF16),
            vmem((8 * HALO, C, V), F32),
            vmem((8 * HALO, C, V), F32),
            vmem((KC, 2 * V), BF16),
            vmem((KC, 2 * V), BF16),
            vmem((KC, 2 * V), BF16),
            vmem((KC, 2 * V), BF16),
            vmem((C, KC), F32),
            vmem((TILES // 2, 2 * C, 2 * V), BF16),
            vmem((ENTRIES, C, V), F32),
            vmem((ENTRIES, C, V), F32),
            vmem((8, RANKS), jnp.int32),
            vmem((8, 128), jnp.int32),
            pltpu.SMEM((8, RANKS), jnp.int32),
            pltpu.SMEM((8, 128), jnp.int32),
            vmem((NB, 32, 128), F32),
            vmem((NB, 32, 128), F32),
            vmem((NB, 32, 128), F32),
            vmem((NB, 32, 128), F32),
            vmem((PLANE, 32, 128), F32),
            vmem((DEEP, 32, 128), F32),
            vmem((NB, 32, 128), F32),
            dma((3,)),
            dma((3,)),
            dma((2,)),
            dma((8,)),
            dma((8,)),
            dma((8,)),
            dma((8,)),
            dma,
            dma,
            dma((NB,)),
            dma((PLANE,)),
            dma((DEEP,)),
            dma((DEEP,)),
            dma((PLANE,)),
            dma((NB,)),
            dma,
            dma,
        ],
        compiler_params=pltpu.CompilerParams(collective_id=0, has_side_effects=True, vmem_limit_bytes=60 << 20),
    )(kernel_map, send_lists, counts, kernel_map, features, weights, cotangent)
    act, gf, gwo = pl.pallas_call(
        finish_kernel,
        out_shape=(shaped((TILES, C, V)), shaped((TILES, C, V)), shaped((OFFS, C, C))),
        in_specs=[SMEM, ANY, ANY, ANY, ANY],
        out_specs=(ANY, ANY, ANY),
        scratch_shapes=[
            vmem((TILES, C, V), F32),
            vmem((TILES, C, V), F32),
            vmem((OFFS, C, C), F32),
            vmem((8 * HALO, C, V), F32),
            vmem((2, NB, 32, 128), F32),
            dma((7,)),
        ],
        compiler_params=pltpu.CompilerParams(vmem_limit_bytes=60 << 20),
    )(send_lists, ge, back, summed, act)
    return act[None, None], gf[None, None], gwo


def solution(mesh):
    placed = (
        P("gx", "gy", None, None, None),
        P(),
        P("gx", "gy", None, None),
        P("gx", "gy", None, None),
        P("gx", "gy"),
        P("gx", "gy", None, None, None),
    )
    return jax.shard_map(
        per_device,
        mesh=mesh,
        in_specs=placed,
        out_specs=(P("gx", "gy", None, None, None), P("gx", "gy", None, None, None), P()),
        check_vma=False,
    )
```
